256 devices in a mesh: dom: 64 (over y, z, core), grp: 4 (over x).
Axes of the slice: x: 4, y: 4, z: 8, core: 2. Of those that a mesh axis runs over, the one named last changes fastest.
Arguments:
- a_tiles: bfloat16 [64, 4, 18, 8, 128, 128], P('dom', 'grp'), as said below
- columns: int32 [64, 4, 18, 8], P('dom', 'grp'), may hold values from 0 to 59, as said below
- surplus_tiles: bfloat16 [64, 4, 6, 8, 128, 128], P('dom', 'grp'), as said below
- surplus_cols: int32 [64, 4, 6, 8], P('dom', 'grp'), may hold values from 0 to 59, as said below
- hosts: int32 [64, 4], P('dom', 'grp'), may hold values from -1 to 2, as said below
- counts: int32 [64, 4], P('dom', 'grp'), may hold values from 6 to 36, as said below
- send_ids: int32 [64, 4, 4, 6], P('dom', 'grp'), may hold values from -1 to 35, as said below
- p0: bfloat16 [64, 4, 36, 96, 128], P('dom', 'grp'), may hold values from -6 to 6
Outputs:
- p_smooth: bfloat16 [64, 4, 36, 96, 128], P('dom', 'grp')
The draws below stay inside these ranges and needn't reach their ends.
Inputs may be any that keep to these rules, and one draw needn't show every extreme that they name: `counts`: in each group of 4 partitions with one dom index, exactly one partition holds 36 tile rows; the others hold 6 to 12. `hosts`: in each group, the partition that holds 36 tile rows has -1; the other three have 0, 1 and 2, each once. send_ids[p, g, j] lists distinct live tile rows of partition (p, g) that partition (p + o_j, g) needs, o = (1, -1, 4, -4); used entries come first and -1 fills the rest; lists toward a partition outside the grid, or for o = 1 or -1 outside the same run of 4 dom indices, are all -1; some list is full in every draw. `columns`: for a live row r below 18 of partition (p, g), slot 0 names r itself; every other slot names a live tile row of the partition or the entry 36 + j * 6 + s for a used entry s of send_ids[p - o_j, g, j]. Other rows name 0 in every slot. `surplus_cols`: for a partition (p, g) with hosts[p, g] = b >= 0, row s describes tile row 18 + b * 6 + s of the group's heaviest partition: slot 0 names that row, every other slot a live tile row of that partition or an entry of its extended list as for columns. The heaviest partition's rows name 0. For a live row r below 18, the diagonal entries of a_tiles[p, g, r, 0] lie between 1 and 2; all tiles of other rows are zero. For a partition with hosts[p, g] >= 0, the diagonal entries of surplus_tiles[p, g, s, 0] lie between 1 and 2; the heaviest partition's surplus_tiles are zero.
All inputs are finite; a program needn't handle non-finite values.
Results may differ from the reference program's by a relative error of at most 0.001.
Values may be sent and summed in bfloat16 or wider, within the bound.
A program may use at most 192 MiB of HBM per device.

```python
import jax
import jax.numpy as jnp
from jax import lax

TB = 128
PC = 96
K = 8
PW = 4
UNIT = 6
RCAP = 36
STORE = 18
DOMAINS = 64
GROUP = 4


def layout(key):
    key_heavy, key_light, key_sizes, key_order, key_slots, key_host = jax.random.split(key, 6)
    members = jnp.arange(GROUP, dtype=jnp.int32)
    heavy_pick = jax.random.randint(key_heavy, (DOMAINS,), 0, GROUP)
    is_heavy = members[None, :] == heavy_pick[:, None]
    light_rows = jax.random.randint(key_light, (DOMAINS, GROUP), UNIT, 2 * UNIT + 1)
    row_counts = jnp.where(is_heavy, 6 * UNIT, light_rows).astype(jnp.int32)
    host_scores = jax.random.randint(key_host, (DOMAINS, GROUP), 0, 1 << 20) * GROUP + members[None, :]
    host_scores = jnp.where(is_heavy, host_scores + (1 << 30), host_scores)
    host_ranks = jnp.argsort(jnp.argsort(host_scores, axis=-1), axis=-1).astype(jnp.int32)
    host_blocks = jnp.where(is_heavy, -1, host_ranks).astype(jnp.int32)
    offsets = jnp.array([1, -1, PW, -PW], dtype=jnp.int32)
    places = jnp.arange(DOMAINS, dtype=jnp.int32)
    receiver = places[:, None] + offsets[None, :]
    inside = (receiver >= 0) & (receiver < DOMAINS)
    same_row = receiver // PW == places[:, None] // PW
    linked = inside & ((jnp.arange(4) >= 2)[None, :] | same_row)
    list_sizes = jax.random.randint(key_sizes, (DOMAINS, GROUP, 4), 1, UNIT + 1)
    list_sizes = jnp.where(linked[:, None, :], list_sizes, 0)
    list_sizes = list_sizes.at[0, :, 0].set(UNIT)
    row_ids = jnp.arange(RCAP, dtype=jnp.int32)
    scores = jax.random.randint(key_order, (DOMAINS, GROUP, 4, RCAP), 0, 1 << 20) * RCAP + row_ids
    scores = jnp.where(row_ids < row_counts[:, :, None, None], scores, scores + (1 << 30))
    ranked = jnp.argsort(scores, axis=-1).astype(jnp.int32)[..., :UNIT]
    entry = jnp.arange(UNIT, dtype=jnp.int32)
    send_lists = jnp.where(entry < list_sizes[..., None], ranked, -1).astype(jnp.int32)
    senders = places[:, None] - offsets[None, :]
    present = (senders >= 0) & (senders < DOMAINS)
    arriving = list_sizes[jnp.clip(senders, 0, DOMAINS - 1), :, jnp.arange(4)[None, :]]
    incoming = jnp.transpose(jnp.where(present[:, :, None], arriving, 0), (0, 2, 1))
    pool = row_counts + jnp.sum(incoming, axis=-1)
    pick = jax.random.randint(key_slots, (DOMAINS, GROUP, RCAP, K), 0, pool[:, :, None, None])
    beyond = pick - row_counts[:, :, None, None]
    ends = jnp.cumsum(incoming, axis=-1)
    starts = ends - incoming
    which = jnp.sum(beyond[..., None] >= ends[:, :, None, None, :], axis=-1)
    first = jnp.sum(jnp.where(jnp.arange(4) == which[..., None], starts[:, :, None, None, :], 0), axis=-1)
    ghost_col = RCAP + which * UNIT + beyond - first
    chosen = jnp.where(beyond < 0, pick, ghost_col)
    slot_ids = jnp.arange(K)[None, None, None, :]
    rows_here = row_ids[None, None, :, None]
    chosen = jnp.where(slot_ids == 0, rows_here, chosen)
    chosen = jnp.where(rows_here < row_counts[:, :, None, None], chosen, 0).astype(jnp.int32)
    heavy_rows = chosen[places, heavy_pick]
    tail_index = STORE + jnp.clip(host_blocks, 0, 2)[:, :, None] * UNIT + entry[None, None, :]
    guest = heavy_rows[places[:, None, None], tail_index]
    guest = jnp.where((host_blocks >= 0)[:, :, None, None], guest, 0).astype(jnp.int32)
    return (row_counts, send_lists, chosen[:, :, :STORE], guest, host_blocks)


def tile_draw(key, rows, live):
    key_mask, key_vals, key_diag = jax.random.split(key, 3)
    full_shape = (DOMAINS, GROUP, rows, K, TB, TB)
    present = jax.random.randint(key_mask, full_shape, 0, 16) == 0
    values = jax.random.normal(key_vals, full_shape, jnp.float32)
    strength = 0.03 * (1.0 + 2.0 * jnp.arange(DOMAINS, dtype=jnp.float32) / (DOMAINS - 1))
    spread = jnp.where(present, values, 0.0) * strength[:, None, None, None, None, None]
    diag_vals = jax.random.uniform(key_diag, (DOMAINS, GROUP, rows, TB), jnp.float32, 1.0, 2.0)
    unit_eye = jnp.eye(TB, dtype=jnp.float32)
    first_slot = (jnp.arange(K) == 0).astype(jnp.float32)[None, None, None, :, None, None]
    on_diag = first_slot * unit_eye
    matrix = spread * (1.0 - on_diag) + on_diag * diag_vals[:, :, :, None, :, None]
    return jnp.where(live[:, :, :, None, None, None], matrix, 0.0)


def draw_counts(key, part):
    return layout(key)[0]


def draw_send_ids(key, part):
    return layout(key)[1]


def draw_columns(key, part):
    return layout(key)[2]


def draw_surplus_cols(key, part):
    return layout(key)[3]


def draw_hosts(key, part):
    return layout(key)[4]


def draw_a_tiles(key, part):
    row_counts = layout(key)[0]
    key = jax.random.fold_in(key, 7)
    live = jnp.arange(STORE)[None, None, :] < row_counts[:, :, None]
    return tile_draw(key, STORE, live).astype(jnp.bfloat16)


def draw_surplus_tiles(key, part):
    host_blocks = layout(key)[4]
    key = jax.random.fold_in(key, 11)
    live = jnp.broadcast_to((host_blocks >= 0)[:, :, None], (DOMAINS, GROUP, UNIT))
    matrix = tile_draw(key, UNIT, live)
    key_dom, key_block, key_row, key_fine, key_dense = jax.random.split(jax.random.fold_in(key, 5), 5)
    lowest = DOMAINS // 2
    plant_dom = jax.random.randint(key_dom, (), lowest, max(DOMAINS - 16, lowest + 1))
    plant_block = jax.random.randint(key_block, (), 0, GROUP - 1)
    members = jnp.arange(GROUP, dtype=jnp.int32)
    plant_member = jnp.sum(jnp.where(host_blocks[plant_dom] == plant_block, members, 0))
    plant_row = jax.random.randint(key_row, (), 0, UNIT)
    plant_fine = jax.random.randint(key_fine, (), 0, TB)
    dense = jax.random.normal(key_dense, (K, TB), jnp.float32)
    dense = 0.03 * dense
    dom_hit = (jnp.arange(DOMAINS) == plant_dom)[:, None, None, None, None, None]
    grp_hit = (members == plant_member)[None, :, None, None, None, None]
    row_hit = (jnp.arange(UNIT) == plant_row)[None, None, :, None, None, None]
    fine_hit = (jnp.arange(TB) == plant_fine)[None, None, None, None, :, None]
    column_hit = (jnp.arange(TB) == plant_fine)[None, None, None, None, None, :]
    slot_ids = jnp.arange(K)[None, None, None, :, None, None]
    target = dom_hit & grp_hit & row_hit & fine_hit
    planted = jnp.where(target & (slot_ids >= 1), dense[None, None, None, :, None, :], matrix)
    planted = jnp.where(target & (slot_ids == 0) & column_hit, 2.0, planted)
    return planted.astype(jnp.bfloat16)


def levels(own_key, extent, shards, smallest, top_value):
    factor_of = 1.0
    for position, shards_of in shards:
        draws = jax.random.uniform(jax.random.fold_in(jax.random.fold_in(own_key, 6), position), (shards_of,), jnp.float32, smallest / len(shards), top_value / len(shards))
        factor_of = factor_of * jnp.repeat(jnp.exp(draws), extent[position] // shards_of).reshape((-1,) + (1,) * (len(extent) - 1 - position))
    return factor_of


def bell_draw(rng, extent, scale, most, shards=(), held_as=jnp.bfloat16):
    entries = jax.random.normal(rng, extent, jnp.float32) * scale
    if len(shards) > 0:
        entries = levels(rng, extent, shards, -0.22, 0.18) * entries
    return jnp.clip(entries, min=-most, max=most).astype(held_as)


def setup_inputs(seed: int = 0) -> dict:
    seeds = jax.random.split(jax.random.key(seed), 9)
    a_tiles = draw_a_tiles(jax.random.fold_in(seeds[8], 71), 0)
    columns = draw_columns(jax.random.fold_in(seeds[8], 71), 0)
    surplus_tiles = draw_surplus_tiles(jax.random.fold_in(seeds[8], 71), 0)
    surplus_cols = draw_surplus_cols(jax.random.fold_in(seeds[8], 71), 0)
    hosts = draw_hosts(jax.random.fold_in(seeds[8], 71), 0)
    counts = draw_counts(jax.random.fold_in(seeds[8], 71), 0)
    send_ids = draw_send_ids(jax.random.fold_in(seeds[8], 71), 0)
    p0 = bell_draw(seeds[7], (DOMAINS, GROUP, RCAP, PC, TB), 1.0, 6.0, ((0, 64), (1, 4)))
    return dict(a_tiles=a_tiles, columns=columns, surplus_tiles=surplus_tiles, surplus_cols=surplus_cols, hosts=hosts, counts=counts, send_ids=send_ids, p0=p0)


def partition_bound(block_tiles, row_count):
    row_ids = jnp.arange(block_tiles.shape[0], dtype=jnp.int32)
    live_rows = row_ids < row_count
    diagonal = jnp.diagonal(block_tiles[:, 0], axis1=1, axis2=2).astype(jnp.float32)
    abs_sums = jnp.sum(jnp.abs(block_tiles.astype(jnp.float32)), axis=(1, 3))
    safe_diag = jnp.where(live_rows[:, None], diagonal, jnp.float32(1.0))
    return jnp.max(jnp.where(live_rows[:, None], abs_sums / safe_diag, jnp.float32(0.0)))


def full_rows(a_tiles, columns, surplus_tiles, surplus_cols, hosts, dom_index, grp_index):
    members = jnp.arange(GROUP, dtype=jnp.int32)
    host_ids = hosts[dom_index]
    holder = jnp.stack([jnp.sum(jnp.where(host_ids == index_b, members, 0)) for index_b in range(GROUP - 1)]).astype(jnp.int32)
    tail_tiles = surplus_tiles[dom_index][holder].reshape((GROUP - 1) * UNIT, K, TB, TB)
    tail_cols = surplus_cols[dom_index][holder].reshape((GROUP - 1) * UNIT, K)
    block_tiles = jnp.concatenate([a_tiles[dom_index, grp_index], tail_tiles], axis=0)
    block_cols = jnp.concatenate([columns[dom_index, grp_index], tail_cols], axis=0)
    return block_tiles, block_cols


def reference(a_tiles, columns, surplus_tiles, surplus_cols, hosts, counts, send_ids, p0):
    offsets = (1, -1, PW, -PW)
    flat_ids = jnp.arange(DOMAINS * GROUP, dtype=jnp.int32)

    def bound_of(index):
        dom_index = index // GROUP
        grp_index = index % GROUP
        block_tiles, block_cols = full_rows(a_tiles, columns, surplus_tiles, surplus_cols, hosts, dom_index, grp_index)
        return partition_bound(block_tiles, counts[dom_index, grp_index])

    largest = jnp.max(lax.map(bound_of, flat_ids))
    damping = 4.0 / (3.0 * largest)

    def smooth(index):
        dom_index = index // GROUP
        grp_index = index % GROUP
        own_p0 = p0[dom_index, grp_index]
        pieces = [own_p0]
        for direction, offset in enumerate(offsets):
            sender = dom_index - offset
            is_valid = (sender >= 0) & (sender < DOMAINS)
            source = jnp.clip(sender, 0, DOMAINS - 1).astype(jnp.int32)
            row_names = send_ids[source, grp_index, direction]
            chosen = p0[source, grp_index][jnp.clip(row_names, 0, RCAP - 1).astype(jnp.int32)]
            keep_mask = is_valid & (row_names >= 0)
            pieces.append(jnp.where(keep_mask[:, None, None], chosen, jnp.zeros_like(chosen)))
        extended = jnp.concatenate(pieces, axis=0)
        block_tiles, block_cols = full_rows(a_tiles, columns, surplus_tiles, surplus_cols, hosts, dom_index, grp_index)
        gathered = extended[block_cols]
        products = jnp.einsum("rkcm,rkim->rci", gathered.astype(jnp.float32), block_tiles.astype(jnp.float32))
        row_ids = jnp.arange(RCAP, dtype=jnp.int32)
        live_rows = row_ids < counts[dom_index, grp_index]
        diagonal = jnp.diagonal(block_tiles[:, 0], axis1=1, axis2=2).astype(jnp.float32)
        inv_diag = 1.0 / jnp.where(live_rows[:, None], diagonal, jnp.float32(1.0))
        result = own_p0.astype(jnp.float32) - damping * inv_diag[:, None, :] * products
        return jnp.where(live_rows[:, None, None], result, jnp.float32(0.0)).astype(jnp.bfloat16)

    smoothed = lax.map(smooth, flat_ids)
    return smoothed.reshape(DOMAINS, GROUP, RCAP, PC, TB)
```

```python
import jax
import jax.numpy as jnp
from jax import lax
from jax.experimental import pallas as pl
from jax.experimental.pallas import tpu as pltpu
from jax.sharding import PartitionSpec as P

MESH = pl.DeviceIdType.MESH
DOM, GRP, PW = 64, 4, 4
Z, Y, CORES = 8, 4, 2
OFFSETS = (1, -1, PW, -PW)
K = 8
UNIT = 6
RCAP = 36
STORE = 18
PC, TB = 96, 128
OWN = RCAP // 2
GHOSTS = len(OFFSETS) * UNIT
SLOTS = OWN + GHOSTS // 2
LAG = 6
STEPS = SLOTS + 2 * LAG
LOADS = 6
ROUNDS = (GRP - 1, Y * CORES - 1, 4, 4)
F32, BF16 = jnp.float32, jnp.bfloat16


def x_peers(p, g):
    return [(p, lax.rem(g + step, GRP)) for step in range(1, GRP)]


def ghost_peers(p, g):
    return [(lax.rem(p + DOM + offset, DOM), g) for offset in OFFSETS]


def plane_peers(p, g):
    core, z, y = lax.rem(p, CORES), lax.rem(lax.div(p, CORES), Z), lax.div(p, CORES * Z)
    return [
        ((lax.rem(y + dy, Y) * Z + z) * CORES + lax.rem(core + dc, CORES), g)
        for dy in range(Y)
        for dc in range(CORES)
        if dy + dc
    ]


def z_peers(p, g):
    core, z, y = lax.rem(p, CORES), lax.rem(lax.div(p, CORES), Z), lax.div(p, CORES * Z)
    return [((y * Z + lax.rem(z + dz, Z)) * CORES + core, g) for dz in (1, Z - 1, 2, Z - 2)]


def remote(source, target, send, recv, device):
    return pltpu.make_async_remote_copy(
        src_ref=source, dst_ref=target, send_sem=send, recv_sem=recv, device_id=device, device_id_type=MESH
    )


def eye():
    return lax.broadcasted_iota(jnp.int32, (TB, TB), 0) == lax.broadcasted_iota(jnp.int32, (TB, TB), 1)


def bound_row(tiles, row, live, top):
    first = tiles[row, 0].astype(F32)
    total = jnp.abs(first)
    for slot in range(1, K):
        total += jnp.abs(tiles[row, slot].astype(F32))
    sums = jnp.sum(total, axis=1, keepdims=True)
    diagonal = jnp.sum(jnp.where(eye(), first, 0.0), axis=1, keepdims=True)
    ratio = sums / jnp.where(live, diagonal, 1.0)
    return jnp.maximum(top, jnp.where(live, ratio, 0.0))


def inverse_diagonal(tiles, row, live):
    diagonal = jnp.sum(jnp.where(eye(), tiles[row, 0].astype(F32), 0.0), axis=0, keepdims=True)
    return 1.0 / jnp.where(live, diagonal, 1.0)


def product(source, names, tiles, row):
    left = jnp.concatenate([source[name] for name in names], axis=1)
    right = jnp.concatenate([tiles[row, slot] for slot in range(K)], axis=1)
    return lax.dot_general(left, right, (((1,), (1,)), ((), ())), preferred_element_type=F32)


def kernel(
    a_hbm, cols, s_hbm, s_cols, hosts, counts, send_ids, p0_hbm, out_hbm,
    a_v, s_v, p_v, ext, picks, moved, got, prods, inverses, outs, guest, back, name_out, names, mine, heard,
    load_sem, move_send, move_recv, ghost_send, ghost_recv, name_send, name_recv, bound_send, bound_recv,
    back_send, back_recv,
):
    p, g = lax.axis_index("dom"), lax.axis_index("grp")
    xs, ghosts, planes, zs = x_peers(p, g), ghost_peers(p, g), plane_peers(p, g), z_peers(p, g)
    right, left = xs[0], xs[-1]

    barrier = pltpu.get_barrier_semaphore()
    greeted = xs + ghosts + planes + zs
    for device in greeted:
        pl.semaphore_signal(barrier, inc=1, device_id=device, device_id_type=MESH)

    p0_copy = pltpu.make_async_copy(p0_hbm.at[0, 0], p_v, load_sem.at[0])
    ext_copy = pltpu.make_async_copy(p0_hbm.at[0, 0], ext.at[pl.ds(0, RCAP)], load_sem.at[1])
    s_copy = pltpu.make_async_copy(s_hbm.at[0, 0], s_v, load_sem.at[2])
    part = STORE // LOADS
    a_copies = [
        pltpu.make_async_copy(
            a_hbm.at[0, 0, pl.ds(i * part, part)], a_v.at[pl.ds(i * part, part)], load_sem.at[3 + i]
        )
        for i in range(LOADS)
    ]
    for copy in (p0_copy, ext_copy, s_copy, *a_copies):
        copy.start()

    block, rows = hosts[0, 0], counts[0, 0]
    heavy = block < 0
    name_out[...] = jnp.full(name_out.shape, block, jnp.int32)

    p0_copy.wait()
    for j in range(len(OFFSETS)):

        def pick(s, carry, j=j):
            picks[j * UNIT + s] = p_v[jnp.maximum(send_ids[0, 0, j, s], 0)]
            return carry

        lax.fori_loop(0, UNIT, pick, 0)
    ext_copy.wait()

    pl.semaphore_wait(barrier, len(greeted))

    ghost_copies = [
        remote(
            picks.at[pl.ds(j * UNIT, UNIT)],
            ext.at[pl.ds(RCAP + j * UNIT, UNIT)],
            ghost_send.at[j],
            ghost_recv.at[j],
            ghosts[j],
        )
        for j in range(len(OFFSETS))
    ]

    def step_copy(way, t, source):
        return remote(
            source,
            got.at[way * STEPS + t],
            move_send.at[way * STEPS + t],
            move_recv.at[way * STEPS + t],
            (right, left)[way],
        )

    def send_own(t):
        for way in range(2):
            step_copy(way, t, ext.at[way * OWN + t]).start()

    def await_step(t):
        for way in range(2):
            step_copy(way, t, got.at[way * STEPS + t]).wait_recv()

    def send_selected(t, base):
        await_step(t - LAG)
        for way in range(2):
            slot = way * SLOTS + t
            moved[slot] = jnp.where(heavy, ext[base[way] + t], got[way * STEPS + t - LAG])
            step_copy(way, t, moved.at[slot]).start()

    def send_forward(t):
        await_step(t - LAG)
        for way in range(2):
            step_copy(way, t, got.at[way * STEPS + t - LAG]).start()

    for t in range(LAG):
        send_own(t)
        if t < len(OFFSETS):
            ghost_copies[t].start()
    name_copies = [
        remote(name_out, names.at[i], name_send.at[i], name_recv.at[i], xs[i]) for i in range(GRP - 1)
    ]
    for copy in name_copies:
        copy.start()

    own_base = (0, OWN)
    ghost_base = (RCAP - OWN, RCAP + GHOSTS // 2 - OWN)

    own_steps = OWN - LAG
    per_step = (STORE + UNIT) // own_steps
    for i in range(LOADS):
        a_copies[i].wait()
    s_copy.wait()
    top = jnp.zeros((TB, 1), F32)

    def stored_step(i, top):
        send_selected(LAG + i, own_base)
        for n in range(per_step):
            row = i * per_step + n
            top = bound_row(a_v, row, row < rows, top)
        return top

    def surplus_step(i, top):
        send_selected(LAG + STORE // per_step + i, own_base)
        for n in range(per_step):
            top = bound_row(s_v, i * per_step + n, block >= 0, top)
        return top

    top = lax.fori_loop(0, STORE // per_step, stored_step, top)
    top = lax.fori_loop(0, UNIT // per_step, surplus_step, top)
    mine[0] = jnp.broadcast_to(jnp.max(top, axis=0, keepdims=True), (8, TB))

    def bound_copies(k):
        base = sum(ROUNDS[:k])
        peers = (xs, planes, zs, zs)[k]
        return [
            remote(mine.at[k], heard.at[base + i], bound_send.at[base + i], bound_recv.at[base + i], peers[i])
            for i in range(ROUNDS[k])
        ]

    def tell(k):
        for copy in bound_copies(k):
            copy.start()

    def hear(k):
        base = sum(ROUNDS[:k])
        for copy in bound_copies(k):
            copy.wait_recv()
        best = mine[k]
        for i in range(ROUNDS[k]):
            best = jnp.maximum(best, heard[base + i])
        mine[k + 1] = best

    tell(0)
    for copy in ghost_copies:
        copy.wait_recv()

    def own_product(row):
        prods[row] = product(ext, [cols[0, 0, row, slot] for slot in range(K)], a_v, row)
        inverses[row] = jnp.broadcast_to(inverse_diagonal(a_v, row, row < rows), (8, TB))

    third = STORE // 3

    def ghost_step(i, carry):
        send_selected(OWN + i, ghost_base)
        own_product(i)
        return carry

    def forward_step(i, carry):
        send_forward(SLOTS + i)
        own_product(2 * third + i)
        return carry

    def last_step(i, carry):
        send_forward(SLOTS + i)
        return carry

    lax.fori_loop(0, third, ghost_step, 0)
    hear(0)
    tell(1)
    lax.fori_loop(third, 2 * third, ghost_step, 0)
    hear(1)
    tell(2)
    lax.fori_loop(0, third, forward_step, 0)
    hear(2)
    tell(3)
    lax.fori_loop(third, 2 * LAG, last_step, 0)
    hear(3)

    damping = 4.0 / (3.0 * mine[4][0:1, :])

    def finish_own(row, carry):
        value = p_v[row].astype(F32) - damping * inverses[row][0:1, :] * prods[row]
        outs[row] = jnp.where(row < rows, value, 0.0).astype(BF16)
        return carry

    lax.fori_loop(0, STORE, finish_own, 0)
    head_copy = pltpu.make_async_copy(
        outs.at[pl.ds(0, STORE)], out_hbm.at[0, 0, pl.ds(0, STORE)], load_sem.at[0]
    )
    head_copy.start()

    for copy in name_copies:
        copy.wait_recv()
    peer_block = [jnp.max(names[i]) for i in range(GRP - 1)]
    away = jnp.int32(1)
    for i in range(1, GRP - 1):
        away = jnp.where(peer_block[i] < 0, i + 1, away)
    shift = (LAG * (away - 1), STEPS + LAG * (GRP - away - 1))

    def place(name):
        ghost = name >= RCAP
        at = jnp.where(ghost, name - RCAP, name)
        span = jnp.where(ghost, GHOSTS // 2, OWN)
        leftward = at >= span
        t = jnp.where(leftward, at - span, at) + jnp.where(ghost, OWN, 0)
        return t + jnp.where(leftward, shift[1], shift[0])

    lax.fori_loop(STEPS - LAG, STEPS, lambda t, carry: (await_step(t), carry)[1], 0)

    def back_copy(s, i):
        return remote(
            guest.at[s],
            back.at[i, s],
            back_send.at[i * UNIT + s],
            back_recv.at[i * UNIT + s],
            xs[i],
        )

    def guest_step(s, carry):
        places = [place(s_cols[0, 0, s, slot]) for slot in range(K)]
        inverse = inverse_diagonal(s_v, s, block >= 0)
        value = got[places[0]].astype(F32) - damping * inverse * product(got, places, s_v, s)
        guest[s] = value.astype(BF16)
        for i in range(GRP - 1):
            back_copy(s, i).start()
        return carry

    lax.fori_loop(0, UNIT, guest_step, 0)

    def drain(t, carry):
        for way in range(2):
            step_copy(way, t, got.at[way * STEPS + t]).wait_send()
        return carry

    lax.fori_loop(0, STEPS, drain, 0)
    for copy in (*ghost_copies, *name_copies):
        copy.wait_send()
    for k in range(len(ROUNDS)):
        for copy in bound_copies(k):
            copy.wait_send()

    def await_back(s, carry):
        for i in range(GRP - 1):
            back_copy(s, i).wait_recv()
        return carry

    lax.fori_loop(0, UNIT, await_back, 0)
    for b in range((RCAP - STORE) // UNIT):
        holder = jnp.int32(0)
        for i in range(GRP - 1):
            holder = jnp.where(peer_block[i] == b, i, holder)

        def finish_tail(s, carry, b=b, holder=holder):
            outs[STORE + b * UNIT + s] = jnp.where(heavy, back[holder, s], jnp.zeros((PC, TB), BF16))
            return carry

        lax.fori_loop(0, UNIT, finish_tail, 0)
    tail_copy = pltpu.make_async_copy(
        outs.at[pl.ds(STORE, RCAP - STORE)], out_hbm.at[0, 0, pl.ds(STORE, RCAP - STORE)], load_sem.at[1]
    )
    tail_copy.start()

    def drain_back(s, carry):
        for i in range(GRP - 1):
            back_copy(s, i).wait_send()
        return carry

    lax.fori_loop(0, UNIT, drain_back, 0)
    head_copy.wait()
    tail_copy.wait()


def on_device(a_tiles, columns, surplus_tiles, surplus_cols, hosts, counts, send_ids, p0):
    smem, anywhere = pl.BlockSpec(memory_space=pltpu.SMEM), pl.BlockSpec(memory_space=pl.ANY)
    dma = pltpu.SemaphoreType.DMA
    tile = (PC, TB)
    return pl.pallas_call(
        kernel,
        out_shape=jax.ShapeDtypeStruct(p0.shape, p0.dtype),
        in_specs=[anywhere, smem, anywhere, smem, smem, smem, smem, anywhere],
        out_specs=anywhere,
        scratch_shapes=[
            pltpu.VMEM((STORE, K, TB, TB), BF16),
            pltpu.VMEM((UNIT, K, TB, TB), BF16),
            pltpu.VMEM((RCAP, *tile), BF16),
            pltpu.VMEM((RCAP + GHOSTS, *tile), BF16),
            pltpu.VMEM((GHOSTS, *tile), BF16),
            pltpu.VMEM((2 * SLOTS, *tile), BF16),
            pltpu.VMEM((2 * STEPS, *tile), BF16),
            pltpu.VMEM((STORE, *tile), F32),
            pltpu.VMEM((STORE, 8, TB), F32),
            pltpu.VMEM((RCAP, *tile), BF16),
            pltpu.VMEM((UNIT, *tile), BF16),
            pltpu.VMEM((GRP - 1, UNIT, *tile), BF16),
            pltpu.VMEM((8, TB), jnp.int32),
            pltpu.VMEM((GRP - 1, 8, TB), jnp.int32),
            pltpu.VMEM((len(ROUNDS) + 1, 8, TB), F32),
            pltpu.VMEM((sum(ROUNDS), 8, TB), F32),
            dma((3 + LOADS,)),
            dma((2 * STEPS,)),
            dma((2 * STEPS,)),
            dma((len(OFFSETS),)),
            dma((len(OFFSETS),)),
            dma((GRP - 1,)),
            dma((GRP - 1,)),
            dma((sum(ROUNDS),)),
            dma((sum(ROUNDS),)),
            dma(((GRP - 1) * UNIT,)),
            dma(((GRP - 1) * UNIT,)),
        ],
        compiler_params=pltpu.CompilerParams(
            collective_id=0, has_side_effects=True, vmem_limit_bytes=40 * 1024 * 1024
        ),
        cost_estimate=pl.CostEstimate(flops=604_000_000, bytes_accessed=9_000_000, transcendentals=0),
    )(a_tiles, columns, surplus_tiles, surplus_cols, hosts, counts, send_ids, p0)


def solution(mesh):
    in_specs = (
        P("dom", "grp", None, None, None, None),
        P("dom", "grp", None, None),
        P("dom", "grp", None, None, None, None),
        P("dom", "grp", None, None),
        P("dom", "grp"),
        P("dom", "grp"),
        P("dom", "grp", None, None),
        P("dom", "grp", None, None, None),
    )
    out_specs = P("dom", "grp", None, None, None)
    return jax.shard_map(on_device, mesh=mesh, in_specs=in_specs, out_specs=out_specs, check_vma=False)
```

```python
import jax
import jax.numpy as jnp
from jax import lax
from jax.experimental import pallas as pl
from jax.experimental.pallas import tpu as pltpu
from jax.sharding import PartitionSpec as P

MESH = pl.DeviceIdType.MESH
DOM, GRP, PW = 64, 4, 4
Z, Y, CORES = 8, 4, 2
OFFSETS = (1, -1, PW, -PW)
K = 8
UNIT = 6
RCAP = 36
STORE = 18
PC, TB = 96, 128
OWN = RCAP // 2
ONE_WAY = OWN + 3 * UNIT // 2
SLOTS = ONE_WAY + UNIT
GHOSTS_AT = (
    ((OWN, UNIT),),
    ((OWN + UNIT, UNIT // 2), (ONE_WAY + OWN, UNIT // 2)),
    ((2 * ONE_WAY, UNIT),),
    ((ONE_WAY + OWN + UNIT // 2, UNIT),),
)
LAG = 7
STEPS = max(ONE_WAY + 2 * LAG, SLOTS + LAG)
LOADS = 6
ROUNDS = (GRP - 1, Y * CORES - 1, 4, 4)
ANSWER_AT, HEAR_AT = (9, None, 12, 17), (13, 20, 32, 41)
VMEM_BYTES = 53 * 1024 * 1024
F32, BF16 = jnp.float32, jnp.bfloat16


def x_peers(p, g):
    return [(p, lax.rem(g + step, GRP)) for step in range(1, GRP)]


def ghost_peers(p, g):
    return [(lax.rem(p + DOM + offset, DOM), g) for offset in OFFSETS]


def linked(p, offset):
    if offset == 1:
        return 1 - lax.div(lax.rem(p, PW), PW - 1)
    if offset == -1:
        return lax.div(lax.rem(p, PW) + PW - 1, PW)
    if offset > 0:
        return 1 - lax.div(p, DOM - PW)
    return lax.div(p + DOM - PW, DOM)


def plane_peers(p, g):
    core, z, y = lax.rem(p, CORES), lax.rem(lax.div(p, CORES), Z), lax.div(p, CORES * Z)
    return [
        ((lax.rem(y + dy, Y) * Z + z) * CORES + lax.rem(core + dc, CORES), g)
        for dy in range(Y)
        for dc in range(CORES)
        if dy + dc
    ]


def z_peers(p, g):
    core, z, y = lax.rem(p, CORES), lax.rem(lax.div(p, CORES), Z), lax.div(p, CORES * Z)
    return [((y * Z + lax.rem(z + dz, Z)) * CORES + core, g) for dz in (1, Z - 1, 2, Z - 2)]


def remote(source, target, send, recv, device):
    return pltpu.make_async_remote_copy(
        src_ref=source, dst_ref=target, send_sem=send, recv_sem=recv, device_id=device, device_id_type=MESH
    )


def eye():
    return lax.broadcasted_iota(jnp.int32, (TB, TB), 0) == lax.broadcasted_iota(jnp.int32, (TB, TB), 1)


def bound_row(tiles, row, live, top):
    first = tiles[row, 0].astype(F32)
    total = jnp.abs(first)
    for slot in range(1, K):
        total += jnp.abs(tiles[row, slot].astype(F32))
    sums = jnp.sum(total, axis=1, keepdims=True)
    diagonal = jnp.sum(jnp.where(eye(), first, 0.0), axis=1, keepdims=True)
    ratio = sums / jnp.where(live, diagonal, 1.0)
    return jnp.maximum(top, jnp.where(live, ratio, 0.0))


def inverse_diagonal(tiles, row, live):
    diagonal = jnp.sum(jnp.where(eye(), tiles[row, 0].astype(F32), 0.0), axis=0, keepdims=True)
    return 1.0 / jnp.where(live, diagonal, 1.0)


def product(source, names, tiles, row):
    left = jnp.concatenate([source[name] for name in names], axis=1)
    right = jnp.concatenate([tiles[row, slot] for slot in range(K)], axis=1)
    return lax.dot_general(left, right, (((1,), (1,)), ((), ())), preferred_element_type=F32)


def position(name):
    shifted = jnp.where(name < RCAP, name + ONE_WAY - OWN, name)
    shifted = jnp.where(name < OWN, name, shifted)
    shifted = jnp.where((name >= RCAP) & (name < 45), name - OWN, shifted)
    shifted = jnp.where((name >= 48) & (name < 54), name + UNIT, shifted)
    return jnp.where(name >= 54, name - UNIT, shifted)


def kernel(
    a_hbm, cols, s_hbm, s_cols, hosts, counts, send_ids, p0_hbm, out,
    a_v, s_v, p_v, ext, picks, moved, got, prods, inverses, guest, back, name_out, names, mine, heard,
    load_sem, move_send, move_recv, ghost_send, ghost_recv, name_send, name_recv, bound_send, bound_recv,
    back_send, back_recv, answer,
):
    p, g = lax.axis_index("dom"), lax.axis_index("grp")
    xs, ghosts, planes, zs = x_peers(p, g), ghost_peers(p, g), plane_peers(p, g), z_peers(p, g)
    right, left = xs[0], xs[-1]

    core, z, y = lax.rem(p, CORES), lax.rem(lax.div(p, CORES), Z), lax.div(p, CORES * Z)
    others = [(ghosts[j], j, linked(p, OFFSETS[j])) for j in range(len(OFFSETS))]
    others += [(device, len(OFFSETS), 1) for device in planes]
    others += [(device, len(OFFSETS) + 1, 1) for device in zs]
    before = []
    for (peer, _), _, there in others:
        peer_core, peer_z, peer_y = lax.rem(peer, CORES), lax.rem(lax.div(peer, CORES), Z), lax.div(peer, CORES * Z)
        mine_is = (z * Y + y) * CORES + core
        before.append((there, lax.div((peer_z * Y + peer_y) * CORES + peer_core + Z * Y * CORES - mine_is, Z * Y * CORES)))
    earlier = [there * is_before for there, is_before in before]
    later = [there * (1 - is_before) for there, is_before in before]
    barrier = pltpu.get_barrier_semaphore()
    for device in xs:
        pl.semaphore_signal(barrier, inc=1, device_id=device, device_id_type=MESH)
    for i, (device, _, _) in enumerate(others):

        @pl.when(earlier[i] == 1)
        def _(device=device):
            pl.semaphore_signal(barrier, inc=1, device_id=device, device_id_type=MESH)

    def load(source, target, i):
        return pltpu.make_async_copy(source, target, load_sem.at[i])

    part = STORE // LOADS
    ext_copies = [
        load(p0_hbm.at[0, 0, pl.ds(way * OWN, OWN)], ext.at[pl.ds(way * ONE_WAY, OWN)], way) for way in range(2)
    ]
    p0_copy = load(p0_hbm.at[0, 0], p_v, 2)
    a_copies = [
        load(a_hbm.at[0, 0, pl.ds(i * part, part)], a_v.at[pl.ds(i * part, part)], 3 + i) for i in range(LOADS)
    ]
    s_copy = load(s_hbm.at[0, 0], s_v, 3 + LOADS)
    for copy in (*ext_copies, p0_copy, *a_copies, s_copy):
        copy.start()

    block, rows = hosts[0, 0], counts[0, 0]
    heavy = block < 0
    name_out[...] = jnp.full(name_out.shape, block, jnp.int32)
    for copy in ext_copies:
        copy.wait()
    pl.semaphore_wait(barrier, GRP - 1 + sum(later))

    def step_copy(way, t, source):
        return remote(
            source,
            got.at[way * STEPS + t],
            move_send.at[way * STEPS + t],
            move_recv.at[way * STEPS + t],
            (right, left)[way],
        )

    def await_step(t):
        for way in range(2):
            step_copy(way, t, got.at[way * STEPS + t]).wait_recv()

    def send_selected(t, base):
        await_step(t - LAG)
        for way in range(2):
            slot = way * SLOTS + t
            moved[slot] = jnp.where(heavy, ext[base[way] + t], got[way * STEPS + t - LAG])
            step_copy(way, t, moved.at[slot]).start()

    def send_forward(t):
        await_step(t - LAG)
        for way in range(2):
            step_copy(way, t, got.at[way * STEPS + t - LAG]).start()

    def one_way(t):
        send_selected(t, (0, ONE_WAY))

    def both_ways(t):
        send_selected(t, (ONE_WAY, ONE_WAY))

    def slots(send, start, end, work=None):
        def step(t, carry):
            send(t)
            if work is not None:
                work(t)
            return carry

        lax.fori_loop(start, end, step, 0)

    for t in range(LAG):
        for way in range(2):
            step_copy(way, t, ext.at[way * ONE_WAY + t]).start()
    name_copies = [
        remote(name_out, names.at[i], name_send.at[i], name_recv.at[i], xs[i]) for i in range(GRP - 1)
    ]
    for copy in name_copies:
        copy.start()

    for i, (device, kind, _) in enumerate(others):
        kind = kind ^ 1 if kind < len(OFFSETS) else kind

        @pl.when(later[i] == 1)
        def _(device=device, kind=kind):
            pl.semaphore_signal(answer.at[kind], inc=1, device_id=device, device_id_type=MESH)

    p0_copy.wait()
    for j in range(len(OFFSETS)):
        for s in range(UNIT):
            picks[j * UNIT + s] = p_v[jnp.maximum(send_ids[0, 0, j, s], 0)]

    def ghost_copy(i, first, count, target, j):
        return remote(
            picks.at[pl.ds(first, count)], ext.at[pl.ds(target, count)], ghost_send.at[i], ghost_recv.at[i], ghosts[j]
        )

    half = UNIT // 2
    ghost_copies = (
        [ghost_copy(0, 0, UNIT, OWN, 0)],
        [ghost_copy(1, UNIT, half, OWN + UNIT, 1), ghost_copy(2, UNIT + half, half, ONE_WAY + OWN, 1)],
        [ghost_copy(3, 2 * UNIT, UNIT, 2 * ONE_WAY, 2)],
        [ghost_copy(4, 3 * UNIT, UNIT, ONE_WAY + OWN + half, 3)],
    )

    for j in (2, 3, 1, 0):

        @pl.when(later[j] == 1)
        def _(j=j):
            for copy in ghost_copies[j]:
                copy.start()

    def await_ghosts(j):
        there = linked(p, -OFFSETS[j])

        @pl.when(there == 1)
        def _():
            for copy in ghost_copies[j]:
                copy.wait_recv()

        @pl.when(there == 0)
        def _():
            for first, count in GHOSTS_AT[j]:
                for s in range(count):
                    ext[first + s] = jnp.zeros((PC, TB), BF16)

    def stored_rows(i, top):
        for n in range(part):
            row = i * part + n
            top = bound_row(a_v, row, row < rows, top)
        return top

    def surplus_rows(i, top):
        for n in range(part):
            top = bound_row(s_v, i * part + n, block >= 0, top)
        return top

    for copy in a_copies:
        copy.wait()
    top = lax.fori_loop(0, LOADS, stored_rows, jnp.zeros((TB, 1), F32))
    s_copy.wait()
    top = lax.fori_loop(0, UNIT // part, surplus_rows, top)
    mine[0] = jnp.broadcast_to(jnp.max(top, axis=0, keepdims=True), (8, TB))

    def bound_copies(k):
        base = sum(ROUNDS[:k])
        peers = (xs, planes, zs, zs)[k]
        return [
            remote(mine.at[k], heard.at[base + i], bound_send.at[base + i], bound_recv.at[base + i], peers[i])
            for i in range(ROUNDS[k])
        ]

    def tell(k):
        if k in (1, 2):
            kind = len(OFFSETS) + k - 1
            answers = sum(n for n, other in zip(earlier, others, strict=True) if other[1] == kind)

            @pl.when(answers > 0)
            def _():
                pl.semaphore_wait(answer.at[kind], answers)

        for copy in bound_copies(k):
            copy.start()

    def hear(k):
        base = sum(ROUNDS[:k])
        for copy in bound_copies(k):
            copy.wait_recv()
        best = mine[k]
        for i in range(ROUNDS[k]):
            best = jnp.maximum(best, heard[base + i])
        mine[k + 1] = best

    def own_product(row):
        names = [position(cols[0, 0, slot, row]) for slot in range(K)]
        prods[row] = product(ext, names, a_v, row)
        inverses[row] = jnp.broadcast_to(inverse_diagonal(a_v, row, row < rows), (8, TB))

    def products(t):
        for n in range(part):
            own_product(part * (t - SLOTS) + n)

    def events(t):
        for j in range(len(OFFSETS)):
            if t == ANSWER_AT[j]:

                @pl.when(earlier[j] == 1)
                def _(j=j):
                    pl.semaphore_wait(answer.at[j], 1)
                    for copy in ghost_copies[j]:
                        copy.start()

        for k in range(len(ROUNDS)):
            if t == HEAR_AT[k]:
                hear(k)
                if k + 1 < len(ROUNDS):
                    tell(k + 1)
        if t == OWN:
            await_ghosts(0)
            await_ghosts(1)
        if t == OWN + half:
            await_ghosts(3)
        if t == ONE_WAY:
            await_ghosts(2)

    tell(0)
    cuts = sorted({LAG, *(t for t in ANSWER_AT if t), *HEAR_AT, OWN, OWN + half, ONE_WAY, SLOTS, SLOTS + LOADS, STEPS})
    cuts = [t for t in cuts if LAG <= t <= STEPS]
    for start, end in zip(cuts, cuts[1:] + [STEPS], strict=True):
        events(start)
        if start < ONE_WAY:
            slots(one_way, start, end)
        elif start < SLOTS:
            slots(both_ways, start, end)
        elif start < STEPS:
            slots(send_forward, start, end, products if start < SLOTS + LOADS else None)

    damping = 4.0 / (3.0 * mine[len(ROUNDS)][0:1, :])
    for row in range(STORE):
        value = p_v[row].astype(F32) - damping * inverses[row][0:1, :] * prods[row]
        out[0, 0, row] = jnp.where(row < rows, value, 0.0).astype(BF16)

    for copy in name_copies:
        copy.wait_recv()
    peer_block = [jnp.max(names[i]) for i in range(GRP - 1)]
    away = jnp.int32(1)
    for i in range(1, GRP - 1):
        away = jnp.where(peer_block[i] < 0, i + 1, away)
    shift = (
        LAG * (away - 1),
        STEPS - ONE_WAY + LAG * (GRP - away - 1),
        jnp.where(away == GRP - 1, STEPS, LAG * (away - 1)) - ONE_WAY,
    )

    def place(name):
        at = position(name)
        return at + jnp.where(at < ONE_WAY, shift[0], jnp.where(at < 2 * ONE_WAY, shift[1], shift[2]))

    def back_copy(n, i):
        rows_of = pl.ds(n * half, half)
        return remote(
            guest.at[rows_of], back.at[i, rows_of], back_send.at[2 * i + n], back_recv.at[2 * i + n], xs[i]
        )

    lax.fori_loop(STEPS - LAG, STEPS, lambda t, carry: (await_step(t), carry)[1], 0)
    for n in range(2):
        for s in range(n * half, (n + 1) * half):
            places = [place(s_cols[0, s, 0, slot]) for slot in range(K)]
            inverse = inverse_diagonal(s_v, s, block >= 0)
            value = got[places[0]].astype(F32) - damping * inverse * product(got, places, s_v, s)
            guest[s] = value.astype(BF16)
        for i in (1, 0, 2):
            back_copy(n, i).start()

    def drain(t, carry):
        for way in range(2):
            step_copy(way, t, got.at[way * STEPS + t]).wait_send()
        return carry

    lax.fori_loop(0, STEPS, drain, 0)
    for copy in name_copies:
        copy.wait_send()
    for j in range(len(OFFSETS)):

        @pl.when(linked(p, OFFSETS[j]) == 1)
        def _(j=j):
            for copy in ghost_copies[j]:
                copy.wait_send()

    for k in range(len(ROUNDS)):
        for copy in bound_copies(k):
            copy.wait_send()

    for n in range(2):
        for i in range(GRP - 1):
            back_copy(n, i).wait_recv()
    for b in range((RCAP - STORE) // UNIT):
        holder = jnp.int32(0)
        for i in range(GRP - 1):
            holder = jnp.where(peer_block[i] == b, i, holder)
        for s in range(UNIT):
            out[0, 0, STORE + b * UNIT + s] = jnp.where(heavy, back[holder, s], jnp.zeros((PC, TB), BF16))
    for n in range(2):
        for i in range(GRP - 1):
            back_copy(n, i).wait_send()


def on_device(a_tiles, columns, surplus_tiles, surplus_cols, hosts, counts, send_ids, p0):
    smem, hbm = pl.BlockSpec(memory_space=pltpu.SMEM), pl.BlockSpec(memory_space=pltpu.HBM)
    dma = pltpu.SemaphoreType.DMA
    tile = (PC, TB)
    return pl.pallas_call(
        kernel,
        out_shape=jax.ShapeDtypeStruct(p0.shape, p0.dtype),
        in_specs=[hbm, smem, hbm, smem, smem, smem, smem, hbm],
        out_specs=pl.BlockSpec(memory_space=pltpu.VMEM),
        scratch_shapes=[
            pltpu.VMEM((STORE, K, TB, TB), BF16),
            pltpu.VMEM((UNIT, K, TB, TB), BF16),
            pltpu.VMEM((RCAP, *tile), BF16),
            pltpu.VMEM((2 * ONE_WAY + UNIT, *tile), BF16),
            pltpu.VMEM((len(OFFSETS) * UNIT, *tile), BF16),
            pltpu.VMEM((2 * SLOTS, *tile), BF16),
            pltpu.VMEM((2 * STEPS, *tile), BF16),
            pltpu.VMEM((STORE, *tile), F32),
            pltpu.VMEM((STORE, 8, TB), F32),
            pltpu.VMEM((UNIT, *tile), BF16),
            pltpu.VMEM((GRP - 1, UNIT, *tile), BF16),
            pltpu.VMEM((8, TB), jnp.int32),
            pltpu.VMEM((GRP - 1, 8, TB), jnp.int32),
            pltpu.VMEM((len(ROUNDS) + 1, 8, TB), F32),
            pltpu.VMEM((sum(ROUNDS), 8, TB), F32),
            dma((4 + LOADS,)),
            dma((2 * STEPS,)),
            dma((2 * STEPS,)),
            dma((5,)),
            dma((5,)),
            dma((GRP - 1,)),
            dma((GRP - 1,)),
            dma((sum(ROUNDS),)),
            dma((sum(ROUNDS),)),
            dma((2 * (GRP - 1),)),
            dma((2 * (GRP - 1),)),
            pltpu.SemaphoreType.REGULAR((len(OFFSETS) + 2,)),
        ],
        compiler_params=pltpu.CompilerParams(
            collective_id=0, has_side_effects=True, vmem_limit_bytes=VMEM_BYTES
        ),
        cost_estimate=pl.CostEstimate(flops=604_000_000, bytes_accessed=9_000_000, transcendentals=0),
    )(
        a_tiles,
        jnp.transpose(columns, (0, 1, 3, 2)),
        surplus_tiles,
        jnp.transpose(surplus_cols, (0, 2, 1, 3)),
        hosts,
        counts,
        send_ids,
        p0,
    )


def solution(mesh):
    in_specs = (
        P("dom", "grp", None, None, None, None),
        P("dom", "grp", None, None),
        P("dom", "grp", None, None, None, None),
        P("dom", "grp", None, None),
        P("dom", "grp"),
        P("dom", "grp"),
        P("dom", "grp", None, None),
        P("dom", "grp", None, None, None),
    )
    out_specs = P("dom", "grp", None, None, None)
    return jax.shard_map(on_device, mesh=mesh, in_specs=in_specs, out_specs=out_specs, check_vma=False)
```

```python
import jax
import jax.numpy as jnp
from jax import lax
from jax.experimental import pallas as pl
from jax.experimental.pallas import tpu as pltpu
from jax.sharding import PartitionSpec as P

MESH = pl.DeviceIdType.MESH
DOM, GRP, PW = 64, 4, 4
Z, Y, CORES = 8, 4, 2
OFFSETS = (1, -1, PW, -PW)
K = 8
UNIT = 6
RCAP = 36
STORE = 18
PC, TB = 96, 128
OWN = RCAP // 2
ONE_WAY = OWN + 3 * UNIT // 2
SLOTS = ONE_WAY + UNIT
GHOSTS_AT = (
    ((OWN, UNIT),),
    ((OWN + UNIT, UNIT // 2), (ONE_WAY + OWN, UNIT // 2)),
    ((2 * ONE_WAY, UNIT),),
    ((ONE_WAY + OWN + UNIT // 2, UNIT),),
)
LAG = 7
STEPS = max(ONE_WAY + 2 * LAG, SLOTS + LAG)
LOADS = 6
ROUNDS = (GRP - 1, Y * CORES - 1, 4, 4)
ANSWER_AT, HEAR_AT = (8, None, 10, 15), (13, 23)
HEAR_Z = ((29, 4, 8), (33, 2, 4), (36, 0, 2))
VMEM_BYTES = 60 * 1024 * 1024
F32, BF16 = jnp.float32, jnp.bfloat16


def x_peers(p, g):
    return [(p, lax.rem(g + step, GRP)) for step in range(1, GRP)]


def ghost_peers(p, g):
    return [(lax.rem(p + DOM + offset, DOM), g) for offset in OFFSETS]


def linked(p, offset):
    if offset == 1:
        return 1 - lax.div(lax.rem(p, PW), PW - 1)
    if offset == -1:
        return lax.div(lax.rem(p, PW) + PW - 1, PW)
    if offset > 0:
        return 1 - lax.div(p, DOM - PW)
    return lax.div(p + DOM - PW, DOM)


def plane_peers(p, g):
    core, z, y = lax.rem(p, CORES), lax.rem(lax.div(p, CORES), Z), lax.div(p, CORES * Z)
    return [
        ((lax.rem(y + dy, Y) * Z + z) * CORES + lax.rem(core + dc, CORES), g)
        for dy in range(Y)
        for dc in range(CORES)
        if dy + dc
    ]


def z_peers(p, g):
    core, z, y = lax.rem(p, CORES), lax.rem(lax.div(p, CORES), Z), lax.div(p, CORES * Z)
    return [((y * Z + lax.rem(z + dz, Z)) * CORES + core, g) for dz in (1, Z - 1, 2, Z - 2)]


def remote(source, target, send, recv, device):
    return pltpu.make_async_remote_copy(
        src_ref=source, dst_ref=target, send_sem=send, recv_sem=recv, device_id=device, device_id_type=MESH
    )


def eye():
    return lax.broadcasted_iota(jnp.int32, (TB, TB), 0) == lax.broadcasted_iota(jnp.int32, (TB, TB), 1)


def bound_row(tiles, row, live, top):
    first = tiles[row, 0].astype(F32)
    total = jnp.abs(first)
    for slot in range(1, K):
        total += jnp.abs(tiles[row, slot].astype(F32))
    sums = jnp.sum(total, axis=1, keepdims=True)
    diagonal = jnp.sum(jnp.where(eye(), first, 0.0), axis=1, keepdims=True)
    ratio = sums / jnp.where(live, diagonal, 1.0)
    return jnp.maximum(top, jnp.where(live, ratio, 0.0))


def inverse_diagonal(tiles, row, live):
    diagonal = jnp.sum(jnp.where(eye(), tiles[row, 0].astype(F32), 0.0), axis=0, keepdims=True)
    return 1.0 / jnp.where(live, diagonal, 1.0)


def product(source, names, tiles, row):
    left = jnp.concatenate([source[name] for name in names], axis=1)
    right = jnp.concatenate([tiles[row, slot] for slot in range(K)], axis=1)
    return lax.dot_general(left, right, (((1,), (1,)), ((), ())), preferred_element_type=F32)


def position(name):
    shifted = jnp.where(name < RCAP, name + ONE_WAY - OWN, name)
    shifted = jnp.where(name < OWN, name, shifted)
    shifted = jnp.where((name >= RCAP) & (name < 45), name - OWN, shifted)
    shifted = jnp.where((name >= 48) & (name < 54), name + UNIT, shifted)
    return jnp.where(name >= 54, name - UNIT, shifted)


def kernel(
    a_hbm, cols_hbm, s_hbm, s_cols_hbm, hosts_hbm, counts_hbm, send_ids_hbm, p0_hbm, out_hbm,
    cols, s_cols, hosts, counts, send_ids, outs,
    a_v, s_v, p_v, ext, picks, moved, got, prods, inverses, guest, back, name_out, names, mine, heard,
    load_sem, move_send, move_recv, ghost_send, ghost_recv, name_send, name_recv, bound_send, bound_recv,
    back_send, back_recv, answer,
):
    p, g = lax.axis_index("dom"), lax.axis_index("grp")
    xs, ghosts, planes, zs = x_peers(p, g), ghost_peers(p, g), plane_peers(p, g), z_peers(p, g)
    right, left = xs[0], xs[-1]

    core, z, y = lax.rem(p, CORES), lax.rem(lax.div(p, CORES), Z), lax.div(p, CORES * Z)
    others = [(ghosts[j], j, linked(p, OFFSETS[j])) for j in range(len(OFFSETS))]
    others += [(device, len(OFFSETS), 1) for device in planes]
    others += [(device, len(OFFSETS) + 1, 1) for device in zs]
    before = []
    for (peer, _), _, there in others:
        peer_core, peer_z, peer_y = lax.rem(peer, CORES), lax.rem(lax.div(peer, CORES), Z), lax.div(peer, CORES * Z)
        mine_is = (z * Y + y) * CORES + core
        before.append((there, lax.div((peer_z * Y + peer_y) * CORES + peer_core + Z * Y * CORES - mine_is, Z * Y * CORES)))
    earlier = [there * is_before for there, is_before in before]
    later = [there * (1 - is_before) for there, is_before in before]
    barrier = pltpu.get_barrier_semaphore()
    for device in xs:
        pl.semaphore_signal(barrier, inc=1, device_id=device, device_id_type=MESH)
    for i, (device, _, _) in enumerate(others):

        @pl.when(earlier[i] == 1)
        def _(device=device):
            pl.semaphore_signal(barrier, inc=1, device_id=device, device_id_type=MESH)

    def load(source, target, i):
        return pltpu.make_async_copy(source, target, load_sem.at[i])

    part = STORE // LOADS
    ext_copies = [
        load(p0_hbm.at[0, 0, pl.ds(way * OWN, OWN)], ext.at[pl.ds(way * ONE_WAY, OWN)], way) for way in range(2)
    ]
    p0_copy = load(p0_hbm.at[0, 0], p_v, 2)
    a_copies = [
        load(a_hbm.at[0, 0, pl.ds(i * part, part)], a_v.at[pl.ds(i * part, part)], 3 + i) for i in range(LOADS)
    ]
    s_copy = load(s_hbm.at[0, 0], s_v, 3 + LOADS)
    integers = (
        (hosts_hbm, hosts),
        (counts_hbm, counts),
        (send_ids_hbm, send_ids),
        (cols_hbm, cols),
        (s_cols_hbm, s_cols),
    )
    integer_copies = [load(*pair, 4 + LOADS + i) for i, pair in enumerate(integers)]
    for copy in (*integer_copies, *ext_copies, p0_copy, *a_copies, s_copy):
        copy.start()

    for copy in integer_copies:
        copy.wait()
    block, rows = hosts[0, 0], counts[0, 0]
    heavy = block < 0
    name_out[...] = jnp.full(name_out.shape, block, jnp.int32)
    for copy in ext_copies:
        copy.wait()
    pl.semaphore_wait(barrier, GRP - 1 + sum(later))

    def step_copy(way, t, source):
        return remote(
            source,
            got.at[way * STEPS + t],
            move_send.at[way * STEPS + t],
            move_recv.at[way * STEPS + t],
            (right, left)[way],
        )

    def await_way(way, t):
        step_copy(way, t, got.at[way * STEPS + t]).wait_recv()

    def await_step(t):
        for way in range(2):
            await_way(way, t)

    def send_selected(t, base):
        for way in range(2):
            await_way(way, t - LAG)
            slot = way * SLOTS + t
            moved[slot] = jnp.where(heavy, ext[base[way] + t], got[way * STEPS + t - LAG])
            step_copy(way, t, moved.at[slot]).start()

    def send_forward(t):
        for way in range(2):
            await_way(way, t - LAG)
            step_copy(way, t, got.at[way * STEPS + t - LAG]).start()

    def one_way(t):
        send_selected(t, (0, ONE_WAY))

    def both_ways(t):
        send_selected(t, (ONE_WAY, ONE_WAY))

    def slots(send, start, end, work=None):
        def step(t, carry):
            send(t)
            if work is not None:
                work(t)
            return carry

        lax.fori_loop(start, end, step, 0)

    for t in range(LAG):
        for way in range(2):
            step_copy(way, t, ext.at[way * ONE_WAY + t]).start()
    name_copies = [
        remote(name_out, names.at[i], name_send.at[i], name_recv.at[i], xs[i]) for i in range(GRP - 1)
    ]
    for copy in name_copies:
        copy.start()

    for i, (device, kind, _) in enumerate(others):
        kind = kind ^ 1 if kind < len(OFFSETS) else kind

        @pl.when(later[i] == 1)
        def _(device=device, kind=kind):
            pl.semaphore_signal(answer.at[kind], inc=1, device_id=device, device_id_type=MESH)

    p0_copy.wait()
    for j in range(len(OFFSETS)):
        for s in range(UNIT):
            picks[j * UNIT + s] = p_v[jnp.maximum(send_ids[0, 0, j, s], 0)]

    def ghost_copy(i, first, count, target, j):
        return remote(
            picks.at[pl.ds(first, count)], ext.at[pl.ds(target, count)], ghost_send.at[i], ghost_recv.at[i], ghosts[j]
        )

    half = UNIT // 2
    ghost_copies = (
        [ghost_copy(0, 0, UNIT, OWN, 0)],
        [ghost_copy(1, UNIT, half, OWN + UNIT, 1), ghost_copy(2, UNIT + half, half, ONE_WAY + OWN, 1)],
        [ghost_copy(3, 2 * UNIT, UNIT, 2 * ONE_WAY, 2)],
        [ghost_copy(4, 3 * UNIT, UNIT, ONE_WAY + OWN + half, 3)],
    )

    for j in (2, 3, 1, 0):

        @pl.when(later[j] == 1)
        def _(j=j):
            for copy in ghost_copies[j]:
                copy.start()

    def await_ghosts(j):
        there = linked(p, -OFFSETS[j])

        @pl.when(there == 1)
        def _():
            for copy in ghost_copies[j]:
                copy.wait_recv()

        @pl.when(there == 0)
        def _():
            for first, count in GHOSTS_AT[j]:
                for s in range(count):
                    ext[first + s] = jnp.zeros((PC, TB), BF16)

    def stored_rows(i, top):
        for n in range(part):
            row = i * part + n
            top = bound_row(a_v, row, row < rows, top)
        return top

    def surplus_rows(i, top):
        for n in range(part):
            top = bound_row(s_v, i * part + n, block >= 0, top)
        return top

    for copy in a_copies:
        copy.wait()
    top = lax.fori_loop(0, LOADS, stored_rows, jnp.zeros((TB, 1), F32))
    s_copy.wait()
    top = lax.fori_loop(0, UNIT // part, surplus_rows, top)
    mine[0] = jnp.broadcast_to(jnp.max(top, axis=0, keepdims=True), (8, TB))

    def bound_copies(k):
        base = sum(ROUNDS[:k])
        peers = (xs, planes, zs, zs)[k]
        return [
            remote(mine.at[k], heard.at[base + i], bound_send.at[base + i], bound_recv.at[base + i], peers[i])
            for i in range(ROUNDS[k])
        ]

    def tell(k):
        if k in (1, 2):
            kind = len(OFFSETS) + k - 1
            answers = sum(n for n, other in zip(earlier, others, strict=True) if other[1] == kind)

            @pl.when(answers > 0)
            def _():
                pl.semaphore_wait(answer.at[kind], answers)

        for copy in bound_copies(k):
            copy.start()

    def hear(k):
        base = sum(ROUNDS[:k])
        for copy in bound_copies(k):
            copy.wait_recv()
        best = mine[k]
        for i in range(ROUNDS[k]):
            best = jnp.maximum(best, heard[base + i])
        mine[k + 1] = best

    def own_product(row):
        names = [position(cols[0, 0, slot, row]) for slot in range(K)]
        prods[row] = product(ext, names, a_v, row)
        inverses[row] = jnp.broadcast_to(inverse_diagonal(a_v, row, row < rows), (8, TB))

    def one_product(t):
        own_product(t - ONE_WAY)

    def two_products(t):
        for n in range(2):
            own_product(UNIT + 2 * (t - SLOTS) + n)

    def events(t):
        for j in range(len(OFFSETS)):
            if t == ANSWER_AT[j]:

                @pl.when(earlier[j] == 1)
                def _(j=j):
                    pl.semaphore_wait(answer.at[j], 1)
                    for copy in ghost_copies[j]:
                        copy.start()

        for k in range(2):
            if t == HEAR_AT[k]:
                hear(k)
                tell(k + 1)
        for at, first, last in HEAR_Z:
            if t == at:

                @pl.when((z >= first) & (z < last))
                def _():
                    hear(2)
                    tell(3)

        if t == OWN:
            await_ghosts(0)
            await_ghosts(1)
        if t == OWN + half:
            await_ghosts(3)
        if t == ONE_WAY:
            await_ghosts(2)

    tell(0)
    cuts = sorted({LAG, *(t for t in ANSWER_AT if t), *HEAR_AT, *(at for at, _, _ in HEAR_Z), OWN, OWN + half, ONE_WAY, SLOTS, SLOTS + UNIT, STEPS})
    cuts = [t for t in cuts if LAG <= t <= STEPS]
    for start, end in zip(cuts, cuts[1:] + [STEPS], strict=True):
        events(start)
        if start < ONE_WAY:
            slots(one_way, start, end)
        elif start < SLOTS:
            slots(both_ways, start, end, one_product)
        elif start < STEPS:
            slots(send_forward, start, end, two_products if start < SLOTS + UNIT else None)

    hear(3)
    damping = 4.0 / (3.0 * mine[len(ROUNDS)][0:1, :])
    for row in range(STORE):
        value = p_v[row].astype(F32) - damping * inverses[row][0:1, :] * prods[row]
        outs[row] = jnp.where(row < rows, value, 0.0).astype(BF16)
    head_copy = load(outs.at[pl.ds(0, STORE)], out_hbm.at[0, 0, pl.ds(0, STORE)], 0)
    head_copy.start()

    for copy in name_copies:
        copy.wait_recv()
    peer_block = [jnp.max(names[i]) for i in range(GRP - 1)]
    away = jnp.int32(1)
    for i in range(1, GRP - 1):
        away = jnp.where(peer_block[i] < 0, i + 1, away)
    shift = (
        LAG * (away - 1),
        STEPS - ONE_WAY + LAG * (GRP - away - 1),
        jnp.where(away == GRP - 1, STEPS, LAG * (away - 1)) - ONE_WAY,
    )

    def place(name):
        at = position(name)
        return at + jnp.where(at < ONE_WAY, shift[0], jnp.where(at < 2 * ONE_WAY, shift[1], shift[2]))

    def back_copy(n, i):
        rows_of = pl.ds(n * half, half)
        return remote(
            guest.at[rows_of], back.at[i, rows_of], back_send.at[2 * i + n], back_recv.at[2 * i + n], xs[i]
        )

    lax.fori_loop(STEPS - LAG, STEPS, lambda t, carry: (await_step(t), carry)[1], 0)
    for n in range(2):
        for s in range(n * half, (n + 1) * half):
            places = [place(s_cols[0, s, 0, slot]) for slot in range(K)]
            inverse = inverse_diagonal(s_v, s, block >= 0)
            value = got[places[0]].astype(F32) - damping * inverse * product(got, places, s_v, s)
            guest[s] = value.astype(BF16)
        for i in (1, 0, 2):
            back_copy(n, i).start()

    def drain(t, carry):
        for way in range(2):
            step_copy(way, t, got.at[way * STEPS + t]).wait_send()
        return carry

    lax.fori_loop(0, STEPS, drain, 0)
    for copy in name_copies:
        copy.wait_send()
    for j in range(len(OFFSETS)):

        @pl.when(linked(p, OFFSETS[j]) == 1)
        def _(j=j):
            for copy in ghost_copies[j]:
                copy.wait_send()

    for k in range(len(ROUNDS)):
        for copy in bound_copies(k):
            copy.wait_send()

    for n in range(2):
        for i in range(GRP - 1):
            back_copy(n, i).wait_recv()
    for b in range((RCAP - STORE) // UNIT):
        holder = jnp.int32(0)
        for i in range(GRP - 1):
            holder = jnp.where(peer_block[i] == b, i, holder)
        for s in range(UNIT):
            outs[STORE + b * UNIT + s] = jnp.where(heavy, back[holder, s], jnp.zeros((PC, TB), BF16))
    tail_copy = load(outs.at[pl.ds(STORE, RCAP - STORE)], out_hbm.at[0, 0, pl.ds(STORE, RCAP - STORE)], 1)
    tail_copy.start()
    for n in range(2):
        for i in range(GRP - 1):
            back_copy(n, i).wait_send()
    head_copy.wait()
    tail_copy.wait()


def hand_over(source, target, held, sem):
    part = RCAP // 2
    rows_of = [pl.ds(i * part, part) for i in range(2)]
    loads = [pltpu.make_async_copy(source.at[0, 0, r], held.at[r], sem.at[i]) for i, r in enumerate(rows_of)]
    stores = [pltpu.make_async_copy(held.at[r], target.at[0, 0, r], sem.at[2 + i]) for i, r in enumerate(rows_of)]
    for copy in loads:
        copy.start()
    for load, store in zip(loads, stores, strict=True):
        load.wait()
        store.start()
    for copy in stores:
        copy.wait()


def on_device(a_tiles, columns, surplus_tiles, surplus_cols, hosts, counts, send_ids, p0):
    hbm = pl.BlockSpec(memory_space=pltpu.HBM)
    dma = pltpu.SemaphoreType.DMA
    tile = (PC, TB)
    smoothed = pl.pallas_call(
        kernel,
        out_shape=jax.ShapeDtypeStruct(p0.shape, p0.dtype),
        in_specs=[hbm] * 8,
        out_specs=hbm,
        scratch_shapes=[
            pltpu.SMEM((1, 1, K, STORE), jnp.int32),
            pltpu.SMEM((1, UNIT, 1, K), jnp.int32),
            pltpu.SMEM((1, 1), jnp.int32),
            pltpu.SMEM((1, 1), jnp.int32),
            pltpu.SMEM((1, 1, len(OFFSETS), UNIT), jnp.int32),
            pltpu.VMEM((RCAP, *tile), BF16),
            pltpu.VMEM((STORE, K, TB, TB), BF16),
            pltpu.VMEM((UNIT, K, TB, TB), BF16),
            pltpu.VMEM((RCAP, *tile), BF16),
            pltpu.VMEM((2 * ONE_WAY + UNIT, *tile), BF16),
            pltpu.VMEM((len(OFFSETS) * UNIT, *tile), BF16),
            pltpu.VMEM((2 * SLOTS, *tile), BF16),
            pltpu.VMEM((2 * STEPS, *tile), BF16),
            pltpu.VMEM((STORE, *tile), F32),
            pltpu.VMEM((STORE, 8, TB), F32),
            pltpu.VMEM((UNIT, *tile), BF16),
            pltpu.VMEM((GRP - 1, UNIT, *tile), BF16),
            pltpu.VMEM((8, TB), jnp.int32),
            pltpu.VMEM((GRP - 1, 8, TB), jnp.int32),
            pltpu.VMEM((len(ROUNDS) + 1, 8, TB), F32),
            pltpu.VMEM((sum(ROUNDS), 8, TB), F32),
            dma((9 + LOADS,)),
            dma((2 * STEPS,)),
            dma((2 * STEPS,)),
            dma((5,)),
            dma((5,)),
            dma((GRP - 1,)),
            dma((GRP - 1,)),
            dma((sum(ROUNDS),)),
            dma((sum(ROUNDS),)),
            dma((2 * (GRP - 1),)),
            dma((2 * (GRP - 1),)),
            pltpu.SemaphoreType.REGULAR((len(OFFSETS) + 2,)),
        ],
        compiler_params=pltpu.CompilerParams(
            collective_id=0, has_side_effects=True, vmem_limit_bytes=VMEM_BYTES
        ),
        cost_estimate=pl.CostEstimate(flops=604_000_000, bytes_accessed=9_000_000, transcendentals=0),
    )(
        a_tiles,
        jnp.transpose(columns, (0, 1, 3, 2)),
        surplus_tiles,
        jnp.transpose(surplus_cols, (0, 2, 1, 3)),
        hosts,
        counts,
        send_ids,
        p0,
    )
    return pl.pallas_call(
        hand_over,
        out_shape=jax.ShapeDtypeStruct(p0.shape, p0.dtype),
        in_specs=[hbm],
        out_specs=hbm,
        scratch_shapes=[pltpu.VMEM((RCAP, *tile), BF16), dma((4,))],
        compiler_params=pltpu.CompilerParams(vmem_limit_bytes=VMEM_BYTES),
    )(smoothed)


def solution(mesh):
    in_specs = (
        P("dom", "grp", None, None, None, None),
        P("dom", "grp", None, None),
        P("dom", "grp", None, None, None, None),
        P("dom", "grp", None, None),
        P("dom", "grp"),
        P("dom", "grp"),
        P("dom", "grp", None, None),
        P("dom", "grp", None, None, None),
    )
    out_specs = P("dom", "grp", None, None, None)
    return jax.shard_map(on_device, mesh=mesh, in_specs=in_specs, out_specs=out_specs, check_vma=False)
```

```python
import jax
import jax.numpy as jnp
from jax import lax
from jax.experimental import pallas as pl
from jax.experimental.pallas import tpu as pltpu
from jax.sharding import PartitionSpec as P

MESH = pl.DeviceIdType.MESH
DOM, GRP, PW = 64, 4, 4
Z, Y, CORES = 8, 4, 2
OFFSETS = (1, -1, PW, -PW)
K = 8
UNIT = 6
RCAP = 36
STORE = 18
PC, TB = 96, 128
OWN = RCAP // 2
ONE_WAY = OWN + 3 * UNIT // 2
SLOTS = ONE_WAY + UNIT
GHOSTS_AT = (
    ((OWN, UNIT),),
    ((ONE_WAY + OWN, UNIT),),
    ((2 * ONE_WAY, UNIT),),
    ((OWN + UNIT, UNIT // 2), (ONE_WAY + OWN + UNIT, UNIT // 2)),
)
LAG = 6
STEPS = max(ONE_WAY + 2 * LAG, SLOTS + LAG)
LOADS = 6
ROUNDS = (GRP - 1, Y * CORES - 1, Z - 1)
ANSWER_AT, HEAR_AT = (8, None, 10, 15), (15, 28)
VMEM_BYTES = 60 * 1024 * 1024
F32, BF16 = jnp.float32, jnp.bfloat16


def x_peers(p, g):
    return [(p, lax.rem(g + step, GRP)) for step in range(1, GRP)]


def ghost_peers(p, g):
    return [(lax.rem(p + DOM + offset, DOM), g) for offset in OFFSETS]


def linked(p, offset):
    if offset == 1:
        return 1 - lax.div(lax.rem(p, PW), PW - 1)
    if offset == -1:
        return lax.div(lax.rem(p, PW) + PW - 1, PW)
    if offset > 0:
        return 1 - lax.div(p, DOM - PW)
    return lax.div(p + DOM - PW, DOM)


def plane_peers(p, g):
    core, z, y = lax.rem(p, CORES), lax.rem(lax.div(p, CORES), Z), lax.div(p, CORES * Z)
    return [
        ((lax.rem(y + dy, Y) * Z + z) * CORES + lax.rem(core + dc, CORES), g)
        for dy in range(Y)
        for dc in range(CORES)
        if dy + dc
    ]


def z_peers(p, g):
    core, z, y = lax.rem(p, CORES), lax.rem(lax.div(p, CORES), Z), lax.div(p, CORES * Z)
    return [((y * Z + lax.rem(z + dz, Z)) * CORES + core, g) for dz in range(1, Z)]


def remote(source, target, send, recv, device):
    return pltpu.make_async_remote_copy(
        src_ref=source, dst_ref=target, send_sem=send, recv_sem=recv, device_id=device, device_id_type=MESH
    )


def eye():
    return lax.broadcasted_iota(jnp.int32, (TB, TB), 0) == lax.broadcasted_iota(jnp.int32, (TB, TB), 1)


def bound_row(tiles, row, live, top):
    first = tiles[row, 0].astype(F32)
    total = jnp.abs(first)
    for slot in range(1, K):
        total += jnp.abs(tiles[row, slot].astype(F32))
    sums = jnp.sum(total, axis=1, keepdims=True)
    diagonal = jnp.sum(jnp.where(eye(), first, 0.0), axis=1, keepdims=True)
    ratio = sums / jnp.where(live, diagonal, 1.0)
    return jnp.maximum(top, jnp.where(live, ratio, 0.0))


def inverse_diagonal(tiles, row, live):
    diagonal = jnp.sum(jnp.where(eye(), tiles[row, 0].astype(F32), 0.0), axis=0, keepdims=True)
    return 1.0 / jnp.where(live, diagonal, 1.0)


def product(source, names, tiles, row):
    left = jnp.concatenate([source[name] for name in names], axis=1)
    right = jnp.concatenate([tiles[row, slot] for slot in range(K)], axis=1)
    return lax.dot_general(left, right, (((1,), (1,)), ((), ())), preferred_element_type=F32)


def position(name):
    shifted = jnp.where(name < RCAP, name + ONE_WAY - OWN, name)
    shifted = jnp.where(name < OWN, name, shifted)
    for first, move in ((RCAP, -OWN), (42, 3), (48, UNIT), (54, -30), (57, -UNIT)):
        shifted = jnp.where(name >= first, name + move, shifted)
    return shifted


def kernel(
    a_hbm, cols_hbm, s_hbm, s_cols_hbm, hosts_hbm, counts_hbm, send_ids_hbm, p0_hbm, out_hbm,
    cols, s_cols, hosts, counts, send_ids, outs,
    a_v, s_v, p_v, ext, picks, moved, got, prods, inverses, guest, back, name_out, names, mine, heard,
    load_sem, move_send, move_recv, ghost_send, ghost_recv, name_send, name_recv, bound_send, bound_recv,
    back_send, back_recv, answer,
):
    p, g = lax.axis_index("dom"), lax.axis_index("grp")
    xs, ghosts, planes, zs = x_peers(p, g), ghost_peers(p, g), plane_peers(p, g), z_peers(p, g)
    right, left = xs[0], xs[-1]

    core, z, y = lax.rem(p, CORES), lax.rem(lax.div(p, CORES), Z), lax.div(p, CORES * Z)
    others = [(ghosts[j], j, linked(p, OFFSETS[j])) for j in range(len(OFFSETS))]
    others += [(device, len(OFFSETS), 1) for device in planes]
    others += [(device, len(OFFSETS) + 1, 1) for device in zs]
    before = []
    for (peer, _), _, there in others:
        peer_core, peer_z, peer_y = lax.rem(peer, CORES), lax.rem(lax.div(peer, CORES), Z), lax.div(peer, CORES * Z)
        mine_is = (z * Y + y) * CORES + core
        before.append((there, lax.div((peer_z * Y + peer_y) * CORES + peer_core + Z * Y * CORES - mine_is, Z * Y * CORES)))
    earlier = [there * is_before for there, is_before in before]
    later = [there * (1 - is_before) for there, is_before in before]
    barrier = pltpu.get_barrier_semaphore()
    for device in xs:
        pl.semaphore_signal(barrier, inc=1, device_id=device, device_id_type=MESH)
    for i, (device, _, _) in enumerate(others):

        @pl.when(earlier[i] == 1)
        def _(device=device):
            pl.semaphore_signal(barrier, inc=1, device_id=device, device_id_type=MESH)

    def load(source, target, i):
        return pltpu.make_async_copy(source, target, load_sem.at[i])

    part = STORE // LOADS
    ext_copies = [
        load(p0_hbm.at[0, 0, pl.ds(way * OWN, OWN)], ext.at[pl.ds(way * ONE_WAY, OWN)], way) for way in range(2)
    ]
    p0_copy = load(p0_hbm.at[0, 0], p_v, 2)
    a_copies = [
        load(a_hbm.at[0, 0, pl.ds(i * part, part)], a_v.at[pl.ds(i * part, part)], 3 + i) for i in range(LOADS)
    ]
    s_copy = load(s_hbm.at[0, 0], s_v, 3 + LOADS)
    integers = (
        (hosts_hbm, hosts),
        (counts_hbm, counts),
        (send_ids_hbm, send_ids),
        (cols_hbm, cols),
        (s_cols_hbm, s_cols),
    )
    integer_copies = [load(*pair, 4 + LOADS + i) for i, pair in enumerate(integers)]
    for copy in (*integer_copies, *ext_copies, p0_copy, *a_copies, s_copy):
        copy.start()

    for copy in integer_copies:
        copy.wait()
    block, rows = hosts[0, 0], counts[0, 0]
    heavy = block < 0
    name_out[...] = jnp.full(name_out.shape, block, jnp.int32)
    for copy in ext_copies:
        copy.wait()
    def say(first, last):
        for i, (device, kind, _) in list(enumerate(others))[first:last]:
            kind = kind ^ 1 if kind < len(OFFSETS) else kind

            @pl.when(later[i] == 1)
            def _(device=device, kind=kind):
                pl.semaphore_signal(answer.at[kind], inc=1, device_id=device, device_id_type=MESH)

    pl.semaphore_wait(barrier, GRP - 1 + sum(later))
    say(0, len(OFFSETS))

    def step_copy(way, t, source):
        return remote(
            source,
            got.at[way * STEPS + t],
            move_send.at[way * STEPS + t],
            move_recv.at[way * STEPS + t],
            (right, left)[way],
        )

    def await_way(way, t):
        step_copy(way, t, got.at[way * STEPS + t]).wait_recv()

    def await_step(t):
        for way in range(2):
            await_way(way, t)

    def send_selected(t, base):
        for way in range(2):
            await_way(way, t - LAG)
            slot = way * SLOTS + t
            moved[slot] = jnp.where(heavy, ext[base[way] + t], got[way * STEPS + t - LAG])
            step_copy(way, t, moved.at[slot]).start()

    def send_forward(t):
        for way in range(2):
            await_way(way, t - LAG)
            step_copy(way, t, got.at[way * STEPS + t - LAG]).start()

    def one_way(t):
        send_selected(t, (0, ONE_WAY))

    def both_ways(t):
        send_selected(t, (ONE_WAY, ONE_WAY))

    def slots(send, start, end, work=None):
        def step(t, carry):
            send(t)
            if work is not None:
                work(t)
            return carry

        lax.fori_loop(start, end, step, 0)

    for t in range(LAG):
        for way in range(2):
            step_copy(way, t, ext.at[way * ONE_WAY + t]).start()
    name_copies = [
        remote(name_out, names.at[i], name_send.at[i], name_recv.at[i], xs[i]) for i in range(GRP - 1)
    ]
    for copy in name_copies:
        copy.start()

    say(len(OFFSETS), len(others))
    p0_copy.wait()
    for j in range(len(OFFSETS)):
        for s in range(UNIT):
            picks[j * UNIT + s] = p_v[jnp.maximum(send_ids[0, 0, j, s], 0)]

    def ghost_copy(i, first, count, target, j):
        return remote(
            picks.at[pl.ds(first, count)], ext.at[pl.ds(target, count)], ghost_send.at[i], ghost_recv.at[i], ghosts[j]
        )

    half = UNIT // 2
    ghost_copies = (
        [ghost_copy(0, 0, UNIT, OWN, 0)],
        [ghost_copy(1, UNIT, UNIT, ONE_WAY + OWN, 1)],
        [ghost_copy(2, 2 * UNIT, UNIT, 2 * ONE_WAY, 2)],
        [
            ghost_copy(3, 3 * UNIT, half, OWN + UNIT, 3),
            ghost_copy(4, 3 * UNIT + half, half, ONE_WAY + OWN + UNIT, 3),
        ],
    )

    for j in (1, 0, 3, 2):

        @pl.when(later[j] == 1)
        def _(j=j):
            for copy in ghost_copies[j]:
                copy.start()

    def await_ghosts(j):
        there = linked(p, -OFFSETS[j])

        @pl.when(there == 1)
        def _():
            for copy in ghost_copies[j]:
                copy.wait_recv()

        @pl.when(there == 0)
        def _():
            for first, count in GHOSTS_AT[j]:
                for s in range(count):
                    ext[first + s] = jnp.zeros((PC, TB), BF16)

    def stored_rows(i, top):
        for n in range(part):
            row = i * part + n
            top = bound_row(a_v, row, row < rows, top)
        return top

    def surplus_rows(i, top):
        for n in range(part):
            top = bound_row(s_v, i * part + n, block >= 0, top)
        return top

    for copy in a_copies:
        copy.wait()
    top = lax.fori_loop(0, LOADS, stored_rows, jnp.zeros((TB, 1), F32))
    s_copy.wait()
    top = lax.fori_loop(0, UNIT // part, surplus_rows, top)
    mine[0] = jnp.broadcast_to(jnp.max(top, axis=0, keepdims=True), (8, TB))

    def bound_copies(k):
        base = sum(ROUNDS[:k])
        peers = (xs, planes, zs)[k]
        return [
            remote(mine.at[k], heard.at[base + i], bound_send.at[base + i], bound_recv.at[base + i], peers[i])
            for i in range(ROUNDS[k])
        ]

    def tell(k):
        if k in (1, 2):
            kind = len(OFFSETS) + k - 1
            answers = sum(n for n, other in zip(earlier, others, strict=True) if other[1] == kind)

            @pl.when(answers > 0)
            def _():
                pl.semaphore_wait(answer.at[kind], answers)

        for copy in bound_copies(k):
            copy.start()

    def hear(k):
        base = sum(ROUNDS[:k])
        for copy in bound_copies(k):
            copy.wait_recv()
        best = mine[k]
        for i in range(ROUNDS[k]):
            best = jnp.maximum(best, heard[base + i])
        mine[k + 1] = best

    def own_product(row):
        names = [position(cols[0, 0, slot, row]) for slot in range(K)]
        prods[row] = product(ext, names, a_v, row)
        inverses[row] = jnp.broadcast_to(inverse_diagonal(a_v, row, row < rows), (8, TB))

    def one_product(t):
        own_product(t - ONE_WAY)

    def two_products(t):
        for n in range(2):
            own_product(UNIT + 2 * (t - SLOTS) + n)

    def events(t):
        for j in range(len(OFFSETS)):
            if t == ANSWER_AT[j]:

                @pl.when(earlier[j] == 1)
                def _(j=j):
                    pl.semaphore_wait(answer.at[j], 1)
                    for copy in ghost_copies[j]:
                        copy.start()

        for k in range(2):
            if t == HEAR_AT[k]:
                hear(k)
                tell(k + 1)
        if t == OWN:
            await_ghosts(0)
            await_ghosts(1)
        if t == OWN + UNIT:
            await_ghosts(3)
        if t == ONE_WAY:
            await_ghosts(2)

    tell(0)
    cuts = sorted({LAG, *(t for t in ANSWER_AT if t), *HEAR_AT, OWN, OWN + UNIT, ONE_WAY, SLOTS, SLOTS + UNIT, STEPS})
    cuts = [t for t in cuts if LAG <= t <= STEPS]
    for start, end in zip(cuts, cuts[1:] + [STEPS], strict=True):
        events(start)
        if start < ONE_WAY:
            slots(one_way, start, end)
        elif start < SLOTS:
            slots(both_ways, start, end, one_product)
        elif start < STEPS:
            slots(send_forward, start, end, two_products if start < SLOTS + UNIT else None)

    hear(2)
    damping = 4.0 / (3.0 * mine[len(ROUNDS)][0:1, :])
    for row in range(STORE):
        value = p_v[row].astype(F32) - damping * inverses[row][0:1, :] * prods[row]
        outs[row] = jnp.where(row < rows, value, 0.0).astype(BF16)
    head_copy = load(outs.at[pl.ds(0, STORE)], out_hbm.at[0, 0, pl.ds(0, STORE)], 0)
    head_copy.start()

    for copy in name_copies:
        copy.wait_recv()
    peer_block = [jnp.max(names[i]) for i in range(GRP - 1)]
    away = jnp.int32(1)
    for i in range(1, GRP - 1):
        away = jnp.where(peer_block[i] < 0, i + 1, away)
    shift = (
        LAG * (away - 1),
        STEPS - ONE_WAY + LAG * (GRP - away - 1),
        jnp.where(away == GRP - 1, STEPS, LAG * (away - 1)) - ONE_WAY,
    )

    def place(name):
        at = position(name)
        return at + jnp.where(at < ONE_WAY, shift[0], jnp.where(at < 2 * ONE_WAY, shift[1], shift[2]))

    def back_copy(n, i):
        rows_of = pl.ds(n * half, half)
        return remote(
            guest.at[rows_of], back.at[i, rows_of], back_send.at[2 * i + n], back_recv.at[2 * i + n], xs[i]
        )

    lax.fori_loop(STEPS - LAG, STEPS, lambda t, carry: (await_step(t), carry)[1], 0)
    for n in range(2):
        for s in range(n * half, (n + 1) * half):
            places = [place(s_cols[0, s, 0, slot]) for slot in range(K)]
            inverse = inverse_diagonal(s_v, s, block >= 0)
            value = got[places[0]].astype(F32) - damping * inverse * product(got, places, s_v, s)
            guest[s] = value.astype(BF16)
        for i in (1, 0, 2):
            back_copy(n, i).start()

    def drain(t, carry):
        for way in range(2):
            step_copy(way, t, got.at[way * STEPS + t]).wait_send()
        return carry

    lax.fori_loop(0, STEPS, drain, 0)
    for copy in name_copies:
        copy.wait_send()
    for j in range(len(OFFSETS)):

        @pl.when(linked(p, OFFSETS[j]) == 1)
        def _(j=j):
            for copy in ghost_copies[j]:
                copy.wait_send()

    for k in range(len(ROUNDS)):
        for copy in bound_copies(k):
            copy.wait_send()

    for n in range(2):
        for i in range(GRP - 1):
            back_copy(n, i).wait_recv()
    for b in range((RCAP - STORE) // UNIT):
        holder = jnp.int32(0)
        for i in range(GRP - 1):
            holder = jnp.where(peer_block[i] == b, i, holder)
        for s in range(UNIT):
            outs[STORE + b * UNIT + s] = jnp.where(heavy, back[holder, s], jnp.zeros((PC, TB), BF16))
    tail_copy = load(outs.at[pl.ds(STORE, RCAP - STORE)], out_hbm.at[0, 0, pl.ds(STORE, RCAP - STORE)], 1)
    tail_copy.start()
    for n in range(2):
        for i in range(GRP - 1):
            back_copy(n, i).wait_send()
    head_copy.wait()
    tail_copy.wait()


def hand_over(source, target, held, sem):
    part = RCAP // 2
    rows_of = [pl.ds(i * part, part) for i in range(2)]
    loads = [pltpu.make_async_copy(source.at[0, 0, r], held.at[r], sem.at[i]) for i, r in enumerate(rows_of)]
    stores = [pltpu.make_async_copy(held.at[r], target.at[0, 0, r], sem.at[2 + i]) for i, r in enumerate(rows_of)]
    for copy in loads:
        copy.start()
    for load, store in zip(loads, stores, strict=True):
        load.wait()
        store.start()
    for copy in stores:
        copy.wait()


def on_device(a_tiles, columns, surplus_tiles, surplus_cols, hosts, counts, send_ids, p0):
    hbm = pl.BlockSpec(memory_space=pltpu.HBM)
    dma = pltpu.SemaphoreType.DMA
    tile = (PC, TB)
    smoothed = pl.pallas_call(
        kernel,
        out_shape=jax.ShapeDtypeStruct(p0.shape, p0.dtype),
        in_specs=[hbm] * 8,
        out_specs=hbm,
        scratch_shapes=[
            pltpu.SMEM((1, 1, K, STORE), jnp.int32),
            pltpu.SMEM((1, UNIT, 1, K), jnp.int32),
            pltpu.SMEM((1, 1), jnp.int32),
            pltpu.SMEM((1, 1), jnp.int32),
            pltpu.SMEM((1, 1, len(OFFSETS), UNIT), jnp.int32),
            pltpu.VMEM((RCAP, *tile), BF16),
            pltpu.VMEM((STORE, K, TB, TB), BF16),
            pltpu.VMEM((UNIT, K, TB, TB), BF16),
            pltpu.VMEM((RCAP, *tile), BF16),
            pltpu.VMEM((2 * ONE_WAY + UNIT, *tile), BF16),
            pltpu.VMEM((len(OFFSETS) * UNIT, *tile), BF16),
            pltpu.VMEM((2 * SLOTS, *tile), BF16),
            pltpu.VMEM((2 * STEPS, *tile), BF16),
            pltpu.VMEM((STORE, *tile), F32),
            pltpu.VMEM((STORE, 8, TB), F32),
            pltpu.VMEM((UNIT, *tile), BF16),
            pltpu.VMEM((GRP - 1, UNIT, *tile), BF16),
            pltpu.VMEM((8, TB), jnp.int32),
            pltpu.VMEM((GRP - 1, 8, TB), jnp.int32),
            pltpu.VMEM((len(ROUNDS) + 1, 8, TB), F32),
            pltpu.VMEM((sum(ROUNDS), 8, TB), F32),
            dma((9 + LOADS,)),
            dma((2 * STEPS,)),
            dma((2 * STEPS,)),
            dma((5,)),
            dma((5,)),
            dma((GRP - 1,)),
            dma((GRP - 1,)),
            dma((sum(ROUNDS),)),
            dma((sum(ROUNDS),)),
            dma((2 * (GRP - 1),)),
            dma((2 * (GRP - 1),)),
            pltpu.SemaphoreType.REGULAR((len(OFFSETS) + 2,)),
        ],
        compiler_params=pltpu.CompilerParams(
            collective_id=0, has_side_effects=True, vmem_limit_bytes=VMEM_BYTES
        ),
        cost_estimate=pl.CostEstimate(flops=604_000_000, bytes_accessed=9_000_000, transcendentals=0),
    )(
        a_tiles,
        jnp.transpose(columns, (0, 1, 3, 2)),
        surplus_tiles,
        jnp.transpose(surplus_cols, (0, 2, 1, 3)),
        hosts,
        counts,
        send_ids,
        p0,
    )
    return pl.pallas_call(
        hand_over,
        out_shape=jax.ShapeDtypeStruct(p0.shape, p0.dtype),
        in_specs=[hbm],
        out_specs=hbm,
        scratch_shapes=[pltpu.VMEM((RCAP, *tile), BF16), dma((4,))],
        compiler_params=pltpu.CompilerParams(vmem_limit_bytes=VMEM_BYTES),
    )(smoothed)


def solution(mesh):
    in_specs = (
        P("dom", "grp", None, None, None, None),
        P("dom", "grp", None, None),
        P("dom", "grp", None, None, None, None),
        P("dom", "grp", None, None),
        P("dom", "grp"),
        P("dom", "grp"),
        P("dom", "grp", None, None),
        P("dom", "grp", None, None, None),
    )
    out_specs = P("dom", "grp", None, None, None)
    return jax.shard_map(on_device, mesh=mesh, in_specs=in_specs, out_specs=out_specs, check_vma=False)
```

```python
import jax
import jax.numpy as jnp
from jax import lax
from jax.experimental import pallas as pl
from jax.experimental.pallas import tpu as pltpu
from jax.sharding import PartitionSpec as P

MESH = pl.DeviceIdType.MESH
DOM, GRP, PW = 64, 4, 4
Z, Y, CORES = 8, 4, 2
OFFSETS = (1, -1, PW, -PW)
K = 8
UNIT = 6
RCAP = 36
STORE = 18
PC, TB = 96, 128
OWN = RCAP // 2
ONE_WAY = OWN + 3 * UNIT // 2
SLOTS = ONE_WAY + UNIT
GHOSTS_AT = (
    ((OWN, UNIT),),
    ((ONE_WAY + OWN, UNIT),),
    ((2 * ONE_WAY, UNIT),),
    ((OWN + UNIT, UNIT // 2), (ONE_WAY + OWN + UNIT, UNIT // 2)),
)
LAG = 6
STEPS = max(ONE_WAY + 2 * LAG, SLOTS + LAG)
LOADS = 6
ROUNDS = (GRP - 1, Y * CORES - 1, Z - 1)
ANSWER_AT, HEAR_AT = (8, None, 10, 15), (15, 28)
VMEM_BYTES = 60 * 1024 * 1024
F32, BF16 = jnp.float32, jnp.bfloat16


def x_peers(p, g):
    return [(p, lax.rem(g + step, GRP)) for step in range(1, GRP)]


def ghost_peers(p, g):
    return [(lax.rem(p + DOM + offset, DOM), g) for offset in OFFSETS]


def linked(p, offset):
    if offset == 1:
        return 1 - lax.div(lax.rem(p, PW), PW - 1)
    if offset == -1:
        return lax.div(lax.rem(p, PW) + PW - 1, PW)
    if offset > 0:
        return 1 - lax.div(p, DOM - PW)
    return lax.div(p + DOM - PW, DOM)


def plane_peers(p, g):
    core, z, y = lax.rem(p, CORES), lax.rem(lax.div(p, CORES), Z), lax.div(p, CORES * Z)
    return [
        ((lax.rem(y + dy, Y) * Z + z) * CORES + lax.rem(core + dc, CORES), g)
        for dy in range(Y)
        for dc in range(CORES)
        if dy + dc
    ]


def z_peers(p, g):
    core, z, y = lax.rem(p, CORES), lax.rem(lax.div(p, CORES), Z), lax.div(p, CORES * Z)
    return [((y * Z + lax.rem(z + dz, Z)) * CORES + core, g) for dz in range(1, Z)]


def remote(source, target, send, recv, device):
    return pltpu.make_async_remote_copy(
        src_ref=source, dst_ref=target, send_sem=send, recv_sem=recv, device_id=device, device_id_type=MESH
    )


def eye():
    return lax.broadcasted_iota(jnp.int32, (TB, TB), 0) == lax.broadcasted_iota(jnp.int32, (TB, TB), 1)


def bound_row(tiles, row, live, top):
    first = tiles[row, 0].astype(F32)
    total = jnp.abs(first)
    for slot in range(1, K):
        total += jnp.abs(tiles[row, slot].astype(F32))
    sums = jnp.sum(total, axis=1, keepdims=True)
    diagonal = jnp.sum(jnp.where(eye(), first, 0.0), axis=1, keepdims=True)
    ratio = sums / jnp.where(live, diagonal, 1.0)
    return jnp.maximum(top, jnp.where(live, ratio, 0.0))


def inverse_diagonal(tiles, row, live):
    diagonal = jnp.sum(jnp.where(eye(), tiles[row, 0].astype(F32), 0.0), axis=0, keepdims=True)
    return 1.0 / jnp.where(live, diagonal, 1.0)


def product(source, names, tiles, row):
    left = jnp.concatenate([source[name] for name in names], axis=1)
    right = jnp.concatenate([tiles[row, slot] for slot in range(K)], axis=1)
    return lax.dot_general(left, right, (((1,), (1,)), ((), ())), preferred_element_type=F32)


def position(name):
    shifted = jnp.where(name < RCAP, name + ONE_WAY - OWN, name)
    shifted = jnp.where(name < OWN, name, shifted)
    for first, move in ((RCAP, -OWN), (42, 3), (48, UNIT), (54, -30), (57, -UNIT)):
        shifted = jnp.where(name >= first, name + move, shifted)
    return shifted


def kernel(
    a_hbm, cols_hbm, s_hbm, s_cols_hbm, hosts_hbm, counts_hbm, send_ids_hbm, p0_hbm, out_hbm,
    cols, s_cols, hosts, counts, send_ids, outs,
    a_v, s_v, p_v, ext, picks, moved, got, prods, inverses, guest, back_first, back_second, name_out, names, mine, heard,
    load_sem, move_send, move_recv, ghost_send, ghost_recv, name_send, name_recv, bound_send, bound_recv,
    back_send, back_recv, answer,
):
    p, g = lax.axis_index("dom"), lax.axis_index("grp")
    xs, ghosts, planes, zs = x_peers(p, g), ghost_peers(p, g), plane_peers(p, g), z_peers(p, g)
    right, left = xs[0], xs[-1]

    core, z, y = lax.rem(p, CORES), lax.rem(lax.div(p, CORES), Z), lax.div(p, CORES * Z)
    others = [(ghosts[j], j, linked(p, OFFSETS[j])) for j in range(len(OFFSETS))]
    others += [(device, len(OFFSETS), 1) for device in planes]
    others += [(device, len(OFFSETS) + 1, 1) for device in zs]
    before = []
    for (peer, _), _, there in others:
        peer_core, peer_z, peer_y = lax.rem(peer, CORES), lax.rem(lax.div(peer, CORES), Z), lax.div(peer, CORES * Z)
        mine_is = (z * Y + y) * CORES + core
        before.append((there, lax.div((peer_z * Y + peer_y) * CORES + peer_core + Z * Y * CORES - mine_is, Z * Y * CORES)))
    earlier = [there * is_before for there, is_before in before]
    later = [there * (1 - is_before) for there, is_before in before]
    barrier = pltpu.get_barrier_semaphore()
    for device in xs:
        pl.semaphore_signal(barrier, inc=1, device_id=device, device_id_type=MESH)
    for i, (device, _, _) in enumerate(others):

        @pl.when(earlier[i] == 1)
        def _(device=device):
            pl.semaphore_signal(barrier, inc=1, device_id=device, device_id_type=MESH)

    def load(source, target, i):
        return pltpu.make_async_copy(source, target, load_sem.at[i])

    part = STORE // LOADS
    ext_copies = [
        load(p0_hbm.at[0, 0, pl.ds(way * OWN, OWN)], ext.at[pl.ds(way * ONE_WAY, OWN)], way) for way in range(2)
    ]
    p0_copy = load(p0_hbm.at[0, 0], p_v, 2)
    a_copies = [
        load(a_hbm.at[0, 0, pl.ds(i * part, part)], a_v.at[pl.ds(i * part, part)], 3 + i) for i in range(LOADS)
    ]
    s_copy = load(s_hbm.at[0, 0], s_v, 3 + LOADS)
    integers = (
        (hosts_hbm, hosts),
        (counts_hbm, counts),
        (send_ids_hbm, send_ids),
        (cols_hbm, cols),
        (s_cols_hbm, s_cols),
    )
    integer_copies = [load(*pair, 4 + LOADS + i) for i, pair in enumerate(integers)]
    for copy in (*integer_copies, *ext_copies, p0_copy, *a_copies, s_copy):
        copy.start()

    for copy in integer_copies:
        copy.wait()
    block, rows = hosts[0, 0], counts[0, 0]
    heavy = block < 0
    name_out[...] = jnp.full(name_out.shape, block, jnp.int32)
    for copy in ext_copies:
        copy.wait()
    def say(first, last):
        for i, (device, kind, _) in list(enumerate(others))[first:last]:
            kind = kind ^ 1 if kind < len(OFFSETS) else kind

            @pl.when(later[i] == 1)
            def _(device=device, kind=kind):
                pl.semaphore_signal(answer.at[kind], inc=1, device_id=device, device_id_type=MESH)

    pl.semaphore_wait(barrier, GRP - 1 + sum(later))
    say(0, len(OFFSETS))

    def step_copy(way, t, source):
        return remote(
            source,
            got.at[way * STEPS + t],
            move_send.at[way * STEPS + t],
            move_recv.at[way * STEPS + t],
            (right, left)[way],
        )

    def await_way(way, t):
        step_copy(way, t, got.at[way * STEPS + t]).wait_recv()

    def await_step(t):
        for way in range(2):
            await_way(way, t)

    def send_selected(t, base):
        for way in range(2):
            await_way(way, t - LAG)
            slot = way * SLOTS + t
            moved[slot] = jnp.where(heavy, ext[base[way] + t], got[way * STEPS + t - LAG])
            step_copy(way, t, moved.at[slot]).start()

    def send_forward(t):
        for way in range(2):
            await_way(way, t - LAG)
            step_copy(way, t, got.at[way * STEPS + t - LAG]).start()

    def one_way(t):
        send_selected(t, (0, ONE_WAY))

    def both_ways(t):
        send_selected(t, (ONE_WAY, ONE_WAY))

    def slots(send, start, end, work=None):
        def step(t, carry):
            send(t)
            if work is not None:
                work(t)
            return carry

        lax.fori_loop(start, end, step, 0)

    for t in range(LAG):
        for way in range(2):
            step_copy(way, t, ext.at[way * ONE_WAY + t]).start()
    name_copies = [
        remote(name_out, names.at[i], name_send.at[i], name_recv.at[i], xs[i]) for i in range(GRP - 1)
    ]
    for copy in name_copies:
        copy.start()

    say(len(OFFSETS), len(others))
    p0_copy.wait()
    for j in range(len(OFFSETS)):
        for s in range(UNIT):
            picks[j * UNIT + s] = p_v[jnp.maximum(send_ids[0, 0, j, s], 0)]

    def ghost_copy(i, first, count, target, j):
        return remote(
            picks.at[pl.ds(first, count)], ext.at[pl.ds(target, count)], ghost_send.at[i], ghost_recv.at[i], ghosts[j]
        )

    half = UNIT // 2
    ghost_copies = (
        [ghost_copy(0, 0, UNIT, OWN, 0)],
        [ghost_copy(1, UNIT, UNIT, ONE_WAY + OWN, 1)],
        [ghost_copy(2, 2 * UNIT, UNIT, 2 * ONE_WAY, 2)],
        [
            ghost_copy(3, 3 * UNIT, half, OWN + UNIT, 3),
            ghost_copy(4, 3 * UNIT + half, half, ONE_WAY + OWN + UNIT, 3),
        ],
    )

    for j in (1, 0, 3, 2):

        @pl.when(later[j] == 1)
        def _(j=j):
            for copy in ghost_copies[j]:
                copy.start()

    def await_ghosts(j):
        there = linked(p, -OFFSETS[j])

        @pl.when(there == 1)
        def _():
            for copy in ghost_copies[j]:
                copy.wait_recv()

        @pl.when(there == 0)
        def _():
            for first, count in GHOSTS_AT[j]:
                for s in range(count):
                    ext[first + s] = jnp.zeros((PC, TB), BF16)

    def stored_rows(i, top):
        for n in range(part):
            row = i * part + n
            top = bound_row(a_v, row, row < rows, top)
        return top

    def surplus_rows(i, top):
        for n in range(part):
            top = bound_row(s_v, i * part + n, block >= 0, top)
        return top

    for copy in a_copies:
        copy.wait()
    top = lax.fori_loop(0, LOADS, stored_rows, jnp.zeros((TB, 1), F32))
    s_copy.wait()
    top = lax.fori_loop(0, UNIT // part, surplus_rows, top)
    mine[0] = jnp.broadcast_to(jnp.max(top, axis=0, keepdims=True), (8, TB))

    def bound_copies(k):
        base = sum(ROUNDS[:k])
        peers = (xs, planes, zs)[k]
        return [
            remote(mine.at[k], heard.at[base + i], bound_send.at[base + i], bound_recv.at[base + i], peers[i])
            for i in range(ROUNDS[k])
        ]

    def tell(k):
        if k in (1, 2):
            kind = len(OFFSETS) + k - 1
            answers = sum(n for n, other in zip(earlier, others, strict=True) if other[1] == kind)

            @pl.when(answers > 0)
            def _():
                pl.semaphore_wait(answer.at[kind], answers)

        for copy in bound_copies(k):
            copy.start()

    def hear(k):
        base = sum(ROUNDS[:k])
        for copy in bound_copies(k):
            copy.wait_recv()
        best = mine[k]
        for i in range(ROUNDS[k]):
            best = jnp.maximum(best, heard[base + i])
        mine[k + 1] = best

    def own_product(row):
        names = [position(cols[0, 0, slot, row]) for slot in range(K)]
        prods[row] = product(ext, names, a_v, row)
        inverses[row] = jnp.broadcast_to(inverse_diagonal(a_v, row, row < rows), (8, TB))

    def one_product(t):
        own_product(t - ONE_WAY)

    def two_products(t):
        for n in range(2):
            own_product(UNIT + 2 * (t - SLOTS) + n)

    def events(t):
        for j in range(len(OFFSETS)):
            if t == ANSWER_AT[j]:

                @pl.when(earlier[j] == 1)
                def _(j=j):
                    pl.semaphore_wait(answer.at[j], 1)
                    for copy in ghost_copies[j]:
                        copy.start()

        for k in range(2):
            if t == HEAR_AT[k]:
                hear(k)
                tell(k + 1)
        if t == OWN:
            await_ghosts(0)
            await_ghosts(1)
        if t == OWN + UNIT:
            await_ghosts(3)
        if t == ONE_WAY:
            await_ghosts(2)

    tell(0)
    cuts = sorted({LAG, *(t for t in ANSWER_AT if t), *HEAR_AT, OWN, OWN + UNIT, ONE_WAY, SLOTS, SLOTS + UNIT, STEPS})
    cuts = [t for t in cuts if LAG <= t <= STEPS]
    for start, end in zip(cuts, cuts[1:] + [STEPS], strict=True):
        events(start)
        if start < ONE_WAY:
            slots(one_way, start, end)
        elif start < SLOTS:
            slots(both_ways, start, end, one_product)
        elif start < STEPS:
            slots(send_forward, start, end, two_products if start < SLOTS + UNIT else None)

    hear(2)
    damping = 4.0 / (3.0 * mine[len(ROUNDS)][0:1, :])
    for copy in name_copies:
        copy.wait_recv()
    peer_block = [jnp.max(names[i]) for i in range(GRP - 1)]
    away = jnp.int32(1)
    for i in range(1, GRP - 1):
        away = jnp.where(peer_block[i] < 0, i + 1, away)
    shift = (
        LAG * (away - 1),
        STEPS - ONE_WAY + LAG * (GRP - away - 1),
        jnp.where(away == GRP - 1, STEPS, LAG * (away - 1)) - ONE_WAY,
    )

    def place(name):
        at = position(name)
        return at + jnp.where(at < ONE_WAY, shift[0], jnp.where(at < 2 * ONE_WAY, shift[1], shift[2]))

    back = (back_first, back_second)

    def back_copy(n, i):
        rows_of = pl.ds(n * half, half)
        return remote(
            guest.at[rows_of], back[n].at[i], back_send.at[2 * i + n], back_recv.at[2 * i + n], xs[i]
        )

    lax.fori_loop(STEPS - LAG, STEPS, lambda t, carry: (await_step(t), carry)[1], 0)
    for n in range(2):
        for s in range(n * half, (n + 1) * half):
            places = [place(s_cols[0, s, 0, slot]) for slot in range(K)]
            inverse = inverse_diagonal(s_v, s, block >= 0)
            value = got[places[0]].astype(F32) - damping * inverse * product(got, places, s_v, s)
            guest[s] = value.astype(BF16)
        for i in (1, 0, 2):
            back_copy(n, i).start()

    for row in range(STORE):
        value = p_v[row].astype(F32) - damping * inverses[row][0:1, :] * prods[row]
        outs[row] = jnp.where(row < rows, value, 0.0).astype(BF16)
    head_copy = load(outs.at[pl.ds(0, STORE)], out_hbm.at[0, 0, pl.ds(0, STORE)], 0)
    head_copy.start()

    def drain(t, carry):
        for way in range(2):
            step_copy(way, t, got.at[way * STEPS + t]).wait_send()
        return carry

    lax.fori_loop(0, STEPS, drain, 0)
    for copy in name_copies:
        copy.wait_send()
    for j in range(len(OFFSETS)):

        @pl.when(linked(p, OFFSETS[j]) == 1)
        def _(j=j):
            for copy in ghost_copies[j]:
                copy.wait_send()

    for k in range(len(ROUNDS)):
        for copy in bound_copies(k):
            copy.wait_send()

    tail_copies = []
    for n in range(2):
        for i in range(GRP - 1):
            back_copy(n, i).wait_recv()
        for b in range((RCAP - STORE) // UNIT):
            holder = jnp.int32(0)
            for i in range(GRP - 1):
                holder = jnp.where(peer_block[i] == b, i, holder)
            first = STORE + b * UNIT + n * half
            for s in range(half):
                outs[first + s] = jnp.where(heavy, back[n][holder, s], jnp.zeros((PC, TB), BF16))
            copy = load(outs.at[pl.ds(first, half)], out_hbm.at[0, 0, pl.ds(first, half)], 1 + len(tail_copies))
            copy.start()
            tail_copies.append(copy)
    for n in range(2):
        for i in range(GRP - 1):
            back_copy(n, i).wait_send()
    head_copy.wait()
    for copy in tail_copies:
        copy.wait()


def hand_over(source, target, held, sem):
    part = RCAP // 2
    rows_of = [pl.ds(i * part, part) for i in range(2)]
    loads = [pltpu.make_async_copy(source.at[0, 0, r], held.at[r], sem.at[i]) for i, r in enumerate(rows_of)]
    stores = [pltpu.make_async_copy(held.at[r], target.at[0, 0, r], sem.at[2 + i]) for i, r in enumerate(rows_of)]
    for copy in loads:
        copy.start()
    for load, store in zip(loads, stores, strict=True):
        load.wait()
        store.start()
    for copy in stores:
        copy.wait()


def on_device(a_tiles, columns, surplus_tiles, surplus_cols, hosts, counts, send_ids, p0):
    hbm = pl.BlockSpec(memory_space=pltpu.HBM)
    dma = pltpu.SemaphoreType.DMA
    tile = (PC, TB)
    smoothed = pl.pallas_call(
        kernel,
        out_shape=jax.ShapeDtypeStruct(p0.shape, p0.dtype),
        in_specs=[hbm] * 8,
        out_specs=hbm,
        scratch_shapes=[
            pltpu.SMEM((1, 1, K, STORE), jnp.int32),
            pltpu.SMEM((1, UNIT, 1, K), jnp.int32),
            pltpu.SMEM((1, 1), jnp.int32),
            pltpu.SMEM((1, 1), jnp.int32),
            pltpu.SMEM((1, 1, len(OFFSETS), UNIT), jnp.int32),
            pltpu.VMEM((RCAP, *tile), BF16),
            pltpu.VMEM((STORE, K, TB, TB), BF16),
            pltpu.VMEM((UNIT, K, TB, TB), BF16),
            pltpu.VMEM((RCAP, *tile), BF16),
            pltpu.VMEM((2 * ONE_WAY + UNIT, *tile), BF16),
            pltpu.VMEM((len(OFFSETS) * UNIT, *tile), BF16),
            pltpu.VMEM((2 * SLOTS, *tile), BF16),
            pltpu.VMEM((2 * STEPS, *tile), BF16),
            pltpu.VMEM((STORE, *tile), F32),
            pltpu.VMEM((STORE, 8, TB), F32),
            pltpu.VMEM((UNIT, *tile), BF16),
            pltpu.VMEM((GRP - 1, UNIT // 2, *tile), BF16),
            pltpu.VMEM((GRP - 1, UNIT // 2, *tile), BF16),
            pltpu.VMEM((8, TB), jnp.int32),
            pltpu.VMEM((GRP - 1, 8, TB), jnp.int32),
            pltpu.VMEM((len(ROUNDS) + 1, 8, TB), F32),
            pltpu.VMEM((sum(ROUNDS), 8, TB), F32),
            dma((9 + LOADS,)),
            dma((2 * STEPS,)),
            dma((2 * STEPS,)),
            dma((5,)),
            dma((5,)),
            dma((GRP - 1,)),
            dma((GRP - 1,)),
            dma((sum(ROUNDS),)),
            dma((sum(ROUNDS),)),
            dma((2 * (GRP - 1),)),
            dma((2 * (GRP - 1),)),
            pltpu.SemaphoreType.REGULAR((len(OFFSETS) + 2,)),
        ],
        compiler_params=pltpu.CompilerParams(
            collective_id=0, has_side_effects=True, vmem_limit_bytes=VMEM_BYTES
        ),
        cost_estimate=pl.CostEstimate(flops=604_000_000, bytes_accessed=9_000_000, transcendentals=0),
    )(
        a_tiles,
        jnp.transpose(columns, (0, 1, 3, 2)),
        surplus_tiles,
        jnp.transpose(surplus_cols, (0, 2, 1, 3)),
        hosts,
        counts,
        send_ids,
        p0,
    )
    return pl.pallas_call(
        hand_over,
        out_shape=jax.ShapeDtypeStruct(p0.shape, p0.dtype),
        in_specs=[hbm],
        out_specs=hbm,
        scratch_shapes=[pltpu.VMEM((RCAP, *tile), BF16), dma((4,))],
        compiler_params=pltpu.CompilerParams(vmem_limit_bytes=VMEM_BYTES),
    )(smoothed)


def solution(mesh):
    in_specs = (
        P("dom", "grp", None, None, None, None),
        P("dom", "grp", None, None),
        P("dom", "grp", None, None, None, None),
        P("dom", "grp", None, None),
        P("dom", "grp"),
        P("dom", "grp"),
        P("dom", "grp", None, None),
        P("dom", "grp", None, None, None),
    )
    out_specs = P("dom", "grp", None, None, None)
    return jax.shard_map(on_device, mesh=mesh, in_specs=in_specs, out_specs=out_specs, check_vma=False)
```
